512 devices in a mesh: span: 32 (over z, core), mesh: 16 (over y, x).
Axes of the slice: x: 4, y: 4, z: 16, core: 2. Of those that a mesh axis runs over, the one named last changes fastest.
Arguments:
- field: float32 [512, 64, 4096], P('span', None, 'mesh'), may hold values from -6 to 6
- coupling: float32 [512, 64, 4096], P('span', None, 'mesh'), may hold values from -0.5 to 0.5
- advect: float32 [2, 64, 4096], P(None, None, 'mesh'), may hold values from -0.04 to 0.04
- send_rows: int32 [16, 16, 31], P('mesh'), may hold values from 0 to 1023, as said below
- neighbours: int32 [4, 4096], P(None, 'mesh'), may hold values from 0 to 1520, as said below
Outputs:
- evolved: float32 [512, 64, 4096], P('span', None, 'mesh')
The draws below stay inside these ranges and needn't reach their ends.
Inputs may be any that keep to these rules, and one draw needn't show every extreme that they name: send_rows[p, q, :] lists first, one per edge shared by devices p and q along mesh, the rows 4 e + f (element e of device p, edge f) whose traces q needs, in the order that q's neighbours refer to; the other entries are 0. Two devices share edges only if their mesh indices differ by one modulo 16; each pair shares at most 31 edges and some pair exactly 31. neighbours[f, e] is a row 4 e' + f' of the element's own device, or 1024 + q * 31 + r for slot r of what device q sends, or 1520 for a wall; edge f meets edge (f + 2) mod 4 of its neighbour; every device has wall edges.
All inputs are finite; a program needn't handle non-finite values.
Results may differ from the reference program's by a relative error of at most 0.0003.
Values sent between devices are 32-bit elements; how exact they have to be, the bound alone decides.
No kernel may reach another device: no remote copies, remote signals or barrier semaphores. Data moves between devices by JAX's collectives and lax.ppermute only.
A program may use at most 64 MiB of HBM per device.

```python
import math
import jax
import jax.numpy as jnp
import numpy as np
from jax import lax

NZ = 512
NODES = 64
ROWS_Y = 16
COLS_DEV = 16
SECTIONS = 2
E_DEV = 256
E_TOT = 4096
CAP = 31
N_MESH = 16


def build_mesh(key):
    base = jax.random.fold_in(key, 7)
    key_order, key_choice, key_slots = jax.random.split(base, 3)
    pattern = (jnp.arange(ROWS_Y) % 2).astype(jnp.int32)
    shuffled = jax.vmap(lambda single: jax.random.permutation(single, pattern))(jax.random.split(key_order, N_MESH))
    chosen = jax.random.randint(key_choice, (), 0, N_MESH)
    offsets = jnp.where((jnp.arange(N_MESH) == chosen)[:, None], pattern[None, :], shuffled).astype(jnp.int32)
    columns = N_MESH * COLS_DEV
    row_index = jnp.arange(ROWS_Y, dtype=jnp.int32)[:, None] * jnp.ones((1, columns), jnp.int32)
    col_index = jnp.ones((ROWS_Y, 1), jnp.int32) * jnp.arange(columns, dtype=jnp.int32)[None, :]
    block = col_index // COLS_DEV
    owner = jnp.where(col_index % COLS_DEV < offsets[block, row_index], (block - 1) % N_MESH, block)
    scores = jax.random.permutation(key_slots, E_TOT).astype(jnp.int32)
    order = jnp.argsort(owner.reshape(-1) * E_TOT + scores)
    position = jnp.zeros((E_TOT,), jnp.int32).at[order].set(jnp.arange(E_TOT, dtype=jnp.int32))
    slot = (position - owner.reshape(-1) * E_DEV).reshape(ROWS_Y, columns)
    changes = (offsets[:, 1:] != offsets[:, :-1]).astype(jnp.int32)
    before = jnp.concatenate([jnp.zeros((N_MESH, 1), jnp.int32), jnp.cumsum(changes, axis=1)], axis=1)
    vertical = jnp.arange(ROWS_Y, dtype=jnp.int32)[None, :] + before
    horizontal = vertical + 1
    wall_link = 4 * E_DEV + N_MESH * CAP
    moves = ((-1, 0), (0, 1), (1, 0), (0, -1))
    send_flat = jnp.zeros((N_MESH * N_MESH * CAP,), jnp.int32)
    links = []
    for edge in range(4):
        step_row, step_col = moves[edge]
        near_row = row_index + step_row
        near_col = (col_index + step_col) % columns
        wall = (near_row < 0) | (near_row >= ROWS_Y)
        safe_row = jnp.clip(near_row, 0, ROWS_Y - 1)
        near_owner = owner[safe_row, near_col]
        near_slot = slot[safe_row, near_col]
        boundary = jnp.where(near_owner == (owner + 1) % N_MESH, near_owner, owner)
        if edge % 2 == 1:
            face = vertical[boundary, row_index]
        elif edge == 0:
            face = horizontal[boundary, jnp.clip(row_index - 1, 0, ROWS_Y - 1)]
        else:
            face = horizontal[boundary, row_index]
        local = 4 * near_slot + (edge + 2) % 4
        remote = 4 * E_DEV + near_owner * CAP + face
        cross = (near_owner != owner) & jnp.logical_not(wall)
        link = jnp.where(wall, wall_link, jnp.where(cross, remote, local))
        links.append(link.reshape(-1))
        target = jnp.where(cross, (owner * N_MESH + near_owner) * CAP + face, N_MESH * N_MESH * CAP)
        send_flat = send_flat.at[target.reshape(-1)].set((4 * slot + edge).reshape(-1), mode='drop')
    by_cell = jnp.stack(links)
    return (send_flat.reshape(N_MESH, N_MESH, CAP), by_cell[:, order].astype(jnp.int32))


def draw_send_rows(key, part):
    return build_mesh(key)[0]


def draw_neighbours(key, part):
    return build_mesh(key)[1]


def steps_of(stream_key, extent, shards, least, largest):
    gain, own = 1.0, jax.random.fold_in(stream_key, 6)
    for dim, shards_of in shards:
        heights = jnp.exp(jax.random.uniform(jax.random.fold_in(own, dim), (shards_of,), jnp.float32, least / len(shards), largest / len(shards)))
        gain = gain * jnp.repeat(heights, extent[dim] // shards_of).reshape([-1 if axis == dim else 1 for axis in range(len(extent))])
    return gain


def normal_values(key, extent, deviation, bound, shards=(), kind=jnp.bfloat16):
    loudness = steps_of(key, extent, shards, -0.22, 0.18) if shards else 1.0
    drawn = jax.random.normal(key, extent, jnp.float32) * deviation * loudness
    return jnp.minimum(jnp.maximum(drawn, -bound), bound).astype(kind)


def setup_inputs(seed: int = 0) -> dict:
    key_of = jax.random.split(jax.random.key(seed), 6)
    return {
        "field": normal_values(key_of[0], (NZ, NODES, E_TOT), 1.0, 6.0, ((0, 32), (2, 16)), jnp.float32),
        "coupling": jnp.clip(jax.random.uniform(key_of[1], (NZ, NODES, E_TOT), jnp.float32, -0.5, 0.5) * steps_of(key_of[1], (NZ, NODES, E_TOT), ((0, 32), (2, 16)), -0.4, 0.0), -0.5, 0.5),
        "advect": jnp.clip(jax.random.uniform(key_of[2], (2, NODES, E_TOT), jnp.float32, -0.04, 0.04) * steps_of(key_of[2], (2, NODES, E_TOT), ((2, 16),), -0.4, 0.0), -0.04, 0.04),
        "send_rows": draw_send_rows(jax.random.fold_in(key_of[5], 71), 0),
        "neighbours": draw_neighbours(jax.random.fold_in(key_of[5], 71), 0),
    }


penalty = 0.3
spread_rate = 0.5

def transform_table(length):
    rows = jnp.arange(length, dtype=jnp.int32)[:, None]
    cols = jnp.arange(length, dtype=jnp.int32)[None, :]
    half = length // 2
    wave = jnp.where(rows <= half, rows, rows - half)
    phase = (wave * cols % length).astype(jnp.float32) * (2.0 * math.pi / length)
    scaled = jnp.where((rows == 0) | (rows == half), 1.0 / math.sqrt(length), math.sqrt(2.0 / length)).astype(jnp.float32)
    return jnp.where(rows <= half, jnp.cos(phase), jnp.sin(phase)) * scaled

def span_factor(first, count, length):
    modes = first + jnp.arange(count, dtype=jnp.int32)
    half = length // 2
    whole_wave = jnp.where(modes <= half, modes, modes - half).astype(jnp.int32)
    wave = whole_wave.astype(jnp.float32)
    smooth = 1.0 - spread_rate * (2.0 * wave / length) ** 2
    return jnp.where(3 * whole_wave <= length, smooth, jnp.zeros_like(smooth))

def derivative_tables():
    index = np.arange(8)
    points = np.cos(np.pi * index / 7.0)
    weights = np.where((index == 0) | (index == 7), 2.0, 1.0) * (-1.0) ** index
    distance = points[:, None] - points[None, :] + np.eye(8)
    matrix = np.outer(weights, 1.0 / weights) / distance * (1.0 - np.eye(8))
    matrix = matrix - np.eye(8) * np.sum(matrix, axis=1)[:, None]
    along_a = np.kron(np.eye(8), matrix)
    along_b = np.kron(matrix, np.eye(8))
    return (jnp.asarray(along_a, dtype=jnp.float32), jnp.asarray(along_b, dtype=jnp.float32))

def apply_table(table, block):
    flat = block.reshape(table.shape[1], -1)
    return jnp.dot(table, flat, precision=lax.Precision.HIGHEST).reshape(block.shape)

def derive(table, block):
    return jnp.einsum('pn,mne->mpe', table, block, precision=lax.Precision.HIGHEST)

def edge_values(block):
    modes, nodes, count = block.shape
    four = block.reshape(modes, 8, 8, count)
    return jnp.stack([four[:, 0], four[:, :, 7], four[:, 7], four[:, :, 0]], axis=1)

def lift_jumps(jump):
    modes = jump.shape[0]
    count = jump.shape[3]
    lifted = jnp.zeros((modes, 8, 8, count), jump.dtype)
    lifted = lifted.at[:, 0, :, :].add(jump[:, 0])
    lifted = lifted.at[:, :, 7, :].add(jump[:, 1])
    lifted = lifted.at[:, 7, :, :].add(jump[:, 2])
    lifted = lifted.at[:, :, 0, :].add(jump[:, 3])
    return lifted.reshape(modes, 64, count)

def operate(spectral, factor, advect, flat_links, along_a, along_b):
    modes, nodes, total = spectral.shape
    own = edge_values(spectral)
    rows = own.transpose(3, 1, 2, 0).reshape(4 * total, 8 * modes)
    table = jnp.concatenate([rows, jnp.zeros((1, 8 * modes), rows.dtype)], axis=0)
    outer = table[flat_links].reshape(total, 4, 8, modes).transpose(3, 1, 2, 0)
    jump = outer - own
    return factor[:, None, None] * spectral + advect[0] * derive(along_a, spectral) + advect[1] * derive(along_b, spectral) + penalty * lift_jumps(jump)

def reference(field, coupling, advect, send_rows, neighbours):
    total = field.shape[2]
    table = transform_table(NZ)
    factor = span_factor(0, NZ, NZ)
    along_a, along_b = derivative_tables()
    owner = jnp.broadcast_to((jnp.arange(total, dtype=jnp.int32) // E_DEV)[None, :], neighbours.shape)
    base_rows = 4 * E_DEV
    offset = neighbours - base_rows
    peer = jnp.clip(offset // CAP, 0, N_MESH - 1).astype(jnp.int32)
    within = (offset % CAP).astype(jnp.int32)
    sent = send_rows[peer, owner, within]
    local_flat = 4 * (owner * E_DEV + neighbours // 4) + neighbours % 4
    remote_flat = 4 * (peer * E_DEV + sent // 4) + sent % 4
    flat_links = jnp.where(neighbours < base_rows, local_flat, remote_flat)
    flat_links = jnp.where(neighbours == base_rows + N_MESH * CAP, 4 * total, flat_links)
    flat_links = flat_links.T.reshape(-1).astype(jnp.int32)
    value = field
    for section in range(SECTIONS):
        mixed = value * (1.0 + coupling)
        spectral = apply_table(table, mixed)
        updated = operate(spectral, factor, advect, flat_links, along_a, along_b)
        value = apply_table(table.T, updated)
    return value
```

```python
import functools

import jax
import jax.numpy as jnp
import numpy as np
from jax import lax
from jax.experimental import pallas as pl
from jax.experimental.pallas import tpu as pltpu
from jax.sharding import PartitionSpec as P


NZ = 512
PLANES = 16
PEN = 0.3
LOW = 128

EDGE_B = (
    [(t, 0) for t in range(8)]
    + [(t, 7) for t in range(8)]
    + [(1, 1)] + [(0, t) for t in range(1, 7)] + [(6, 1)]
    + [(1, 6)] + [(7, t) for t in range(1, 7)] + [(6, 6)]
)
B_NODES = [8 * b + a for a, b in EDGE_B]
I_NODES = [n for n in range(64) if n not in B_NODES]


def split_table(table):
    high = table.astype(jnp.bfloat16)
    low = (table - np.asarray(high, np.float64)).astype(jnp.bfloat16)
    return np.asarray(high), np.asarray(low)


def filter_table():
    wave = np.arange(NZ // 2 + 1)
    keep = np.where(3 * wave <= NZ, 1.0 - 0.5 * (2.0 * wave / NZ) ** 2, 0.0)
    fold = np.where((wave == 0) | (wave == NZ // 2), 1.0, 2.0) / NZ
    lag = np.arange(NZ)
    phase = 2.0 * np.pi * ((wave[:, None] * lag[None, :]) % NZ) / NZ
    row = np.sum((keep * fold)[:, None] * np.cos(phase), axis=0)
    return row[(lag[:, None] - lag[None, :]) % NZ]


def derivative_tables():
    index = np.arange(8)
    points = np.cos(np.pi * index / 7.0)
    weights = np.where((index == 0) | (index == 7), 2.0, 1.0) * (-1.0) ** index
    distance = points[:, None] - points[None, :] + np.eye(8)
    matrix = np.outer(weights, 1.0 / weights) / distance * (1.0 - np.eye(8))
    matrix = matrix - np.eye(8) * np.sum(matrix, axis=1)[:, None]
    return np.kron(np.eye(8), matrix), np.kron(matrix, np.eye(8))


def edge_count():
    count = np.zeros(64)
    for n in range(64):
        a, b = n % 8, n // 8
        count[n] = (a == 0) + (a == 7) + (b == 0) + (b == 7)
    return count


def lane_node(lane):
    which, rest = divmod(lane, 64)
    half, i = divmod(rest, 32)
    return half, (B_NODES if which == 0 else I_NODES)[i]


def order_table():
    table = np.zeros((128, 128))
    for lane in range(128):
        half, node = lane_node(lane)
        table[lane, 64 * half + node] = 1.0
    return table


def lane_tables():
    along_a, along_b = derivative_tables()
    out = [np.zeros((128, 128)) for _ in range(2)]
    for k, matrix in enumerate((along_a, along_b)):
        for p in range(128):
            for n in range(128):
                hp, np_ = lane_node(p)
                hn, nn = lane_node(n)
                if hp == hn:
                    out[k][n, p] = matrix[np_, nn]
    count = np.array([edge_count()[lane_node(p)[1]] for p in range(128)])
    return out[0], out[1], count


def iota(shape, axis):
    return lax.broadcasted_iota(jnp.int32, shape, axis)


def halves(x):
    high = x.astype(jnp.bfloat16)
    return high, (x - high.astype(jnp.float32)).astype(jnp.bfloat16)


def dot(a, b):
    return jnp.dot(a, b, preferred_element_type=jnp.float32)


def dot3(ah, al, bh, bl):
    return dot(ah, bh) + dot(ah, bl) + dot(al, bh)


def stack_halves(x):
    return jnp.concatenate([x[:, :LOW], x[:, LOW:]], axis=0)


def call(kernel, outs, flops, limit=16):
    def run(*args):
        moved = sum(a.size * a.dtype.itemsize for a in args)
        moved += sum(int(np.prod(o[0])) * 4 for o in outs)
        shapes = [jax.ShapeDtypeStruct(o[0], o[1]) for o in outs]
        result = pl.pallas_call(
            kernel,
            out_shape=shapes if len(shapes) > 1 else shapes[0],
            compiler_params=pltpu.CompilerParams(vmem_limit_bytes=limit * 2**20),
            cost_estimate=pl.CostEstimate(flops=flops, bytes_accessed=moved, transcendentals=0),
        )(*args)
        return result

    return run


def pack_kernel(field_ref, coupling_ref, order_ref, out_ref):
    order = order_ref[...]
    inner = order[64:]
    for j in range(PLANES):
        c = coupling_ref[j]
        x = stack_halves(field_ref[j] * (1.0 + c))
        xh, xl = halves(x)
        out_ref[pl.ds(j, LOW, stride=24), :] = (dot(order, xh) + dot(order, xl)).T
    for j in range(8):
        parts = []
        for up in (0, 8):
            ch, cl = halves(stack_halves(coupling_ref[j + up]))
            parts.append(dot(inner, ch) + dot(inner, cl))
        out_ref[pl.ds(16 + j, LOW, stride=24), :] = jnp.concatenate(parts, axis=0).T


def one_hot_rows(index_ref, width):
    index = index_ref[...]
    hot = iota((index.shape[0], width), 1) == index
    return jnp.where(hot, 1.0, 0.0).astype(jnp.bfloat16)


def one_hot_cols(index_ref, first, count):
    index = index_ref[...]
    hot = (iota((count, index.shape[1]), 0) + first) == index
    return jnp.where(hot, 1.0, 0.0).astype(jnp.bfloat16)


NT = (((1,), (1,)), ((), ()))


def dot_nt(a, b):
    return lax.dot_general(a, b, NT, preferred_element_type=jnp.float32)


def sent(trace, pick_ref, sent_ref):
    th, tl = halves(trace)
    pick = one_hot_rows(pick_ref, 1024)
    sent_ref[...] = dot_nt(pick, th) + dot_nt(pick, tl)


def first_traces_kernel(field_ref, coupling_ref, pick_ref, trace_ref, sent_ref, mixed):
    for j in range(PLANES):
        x = field_ref[j] * (1.0 + coupling_ref[j])
        mixed[0, pl.ds(64 * j, 64), :] = x[:, :LOW]
        mixed[1, pl.ds(64 * j, 64), :] = x[:, LOW:]
        trace_ref[pl.ds(8 * j, 8), pl.ds(0, 256)] = x[:8]
        trace_ref[pl.ds(8 * j, 8), pl.ds(512, 256)] = x[56:]
    for h in range(2):
        trace_ref[:, pl.ds(256 + LOW * h, LOW)] = mixed[h, pl.ds(7, 128, stride=8), :]
        trace_ref[:, pl.ds(768 + LOW * h, LOW)] = mixed[h, pl.ds(0, 128, stride=8), :]
    sent(trace_ref[...], pick_ref, sent_ref)


def outer_traces(trace_ref, came_ref, link_ref):
    th, tl = halves(trace_ref[...])
    ch, cl = halves(came_ref[...].T)
    here = one_hot_cols(link_ref, 0, 1024)
    there = one_hot_cols(link_ref, 1024, 64)
    return dot(th, here) + dot(tl, here) + dot(ch, there) + dot(cl, there)


def lifted(outer):
    f0, f1, f2, f3 = (outer[:, 256 * f : 256 * f + 256].reshape(16, 8, 256) for f in range(4))
    t = iota((16, 8, 256), 1)
    first, last = t == 0, t == 7
    g0 = f0 + jnp.where(first, f3[:, 0:1], 0.0) + jnp.where(last, f1[:, 0:1], 0.0)
    g1 = f2 + jnp.where(first, f3[:, 7:8], 0.0) + jnp.where(last, f1[:, 7:8], 0.0)
    ends = first | last
    return g0, g1, jnp.where(ends, 0.0, f3), jnp.where(ends, 0.0, f1)


def first_local_kernel(
    field_ref, coupling_ref, advect_ref, trace_ref, came_ref, link_ref, near_ref, pick_ref, gain_ref, add_ref, lift
):
    for g, part in enumerate(lifted(outer_traces(trace_ref, came_ref, link_ref))):
        lift[:, pl.ds(8 * g, 8), :] = part * PEN
    near = near_ref[...]
    pick = pick_ref[...]
    ad_a, ad_b = advect_ref[0], advect_ref[1]

    def plane(j):
        c = coupling_ref[j]
        xh, xl = halves(field_ref[j] * (1.0 + c))
        parts = dot(near, jnp.concatenate([xh, xl, xh], axis=0))
        ch, cl = halves(c)
        gain = 1.0 + (dot(pick, ch) + dot(pick, cl))
        local = ad_a * parts[0:32] + ad_b * parts[32:64] + parts[64:96] + lift[j]
        return gain, gain * local

    for j in range(8):
        gains, adds = [], []
        for up in (0, 8):
            gain, add = plane(j + up)
            gains.append(stack_halves(gain))
            adds.append(stack_halves(add))
        gain_ref[pl.ds(j, LOW, stride=8), :] = jnp.concatenate(gains, axis=0).T
        add_ref[pl.ds(j, LOW, stride=8), :] = jnp.concatenate(adds, axis=0).T


def second_traces_kernel(value_ref, pick_ref, trace_ref, sent_ref):
    t = iota((8, 256), 0)
    for j in range(8):
        rows = value_ref[pl.ds(j, LOW, stride=8), :].T
        for up in range(2):
            part = rows[64 * up : 64 * up + 64]
            g = [
                jnp.concatenate([part[8 * k : 8 * k + 8], part[32 + 8 * k : 40 + 8 * k]], axis=1) for k in range(4)
            ]
            f3 = jnp.where(t == 0, g[0][0:1], jnp.where(t == 7, g[1][0:1], g[2]))
            f1 = jnp.where(t == 0, g[0][7:8], jnp.where(t == 7, g[1][7:8], g[3]))
            for f, one in enumerate((g[0], f1, g[1], f3)):
                trace_ref[pl.ds(8 * (j + 8 * up), 8), pl.ds(256 * f, 256)] = one
    sent(trace_ref[...], pick_ref, sent_ref)


def second_local_kernel(trace_ref, came_ref, link_ref, lift_ref):
    for g, part in enumerate(lifted(outer_traces(trace_ref, came_ref, link_ref))):
        lift_ref[:, pl.ds(8 * g, 8), :] = part * PEN


def final_kernel(value_ref, lift_ref, back_ref, out_ref):
    back = back_ref[...]
    for j in range(PLANES):
        rows = value_ref[pl.ds(j, LOW, stride=16), :].T
        edge = rows[:64] + stack_halves(lift_ref[j])
        rows = jnp.concatenate([edge, rows[64:]], axis=0)
        rh, rl = halves(rows)
        full = dot(back, rh) + dot(back, rl)
        out_ref[j] = jnp.concatenate([full[:64], full[64:]], axis=1)


def lanes_swapped(x):
    return pltpu.roll(x, 64, x.ndim - 1)


def first_filter_kernel(value_ref, high_ref, low_ref, edge_ref, inner_ref):
    low_lanes = iota((32, 8, LOW), 2) < 64
    for pair in range(2):
        xs = [value_ref[:, 2 * pair + k, pl.ds(0, 16), :].reshape(NZ, LOW) for k in range(2)]
        xh, xl = halves(jnp.concatenate(xs, axis=1))
        y = dot3(high_ref[...], low_ref[...], xh, xl)
        for k in range(2):
            e = 2 * pair + k
            rows = y[:, LOW * k : LOW * k + LOW].reshape(32, 16, LOW)
            up, down = rows[:, :8], rows[:, 8:]
            edge_ref[:, e] = jnp.where(low_lanes, up, lanes_swapped(down.reshape(256, LOW)).reshape(32, 8, LOW))
            inner_ref[:, e] = jnp.where(low_lanes, lanes_swapped(up.reshape(256, LOW)).reshape(32, 8, LOW), down)


def first_inner_kernel(value_ref, inner_ref, slope_ref, advect_ref, out_ref):
    low_lanes = iota((32, 8, LOW), 2) < 64
    slope = slope_ref[...]
    for e in range(4):
        xh, xl = halves(value_ref[:, e, pl.ds(0, 16), :].reshape(NZ, LOW))
        u = dot(jnp.concatenate([xh, xl, xh], axis=1), slope) * advect_ref[pl.ds(e, 1), :]
        v = (u + lanes_swapped(u)).reshape(32, 16, LOW)
        local = jnp.where(low_lanes, v[:, :8], v[:, 8:])
        out_ref[:, e] = (inner_ref[:, e] + local) * (1.0 + value_ref[:, e, pl.ds(16, 8), :])


def second_filter_kernel(edge_ref, inner_ref, high_ref, low_ref, slope_ref, advect_ref, count_ref, out_ref):
    low_lanes = iota((32, 8, LOW), 2) < 64
    slope = slope_ref[...]
    count = count_ref[...]
    for pair in range(2):
        xs = []
        for k in range(2):
            e = 2 * pair + k
            edge, inner = edge_ref[:, e], inner_ref[:, e]
            up = jnp.where(low_lanes, edge, lanes_swapped(inner.reshape(256, LOW)).reshape(32, 8, LOW))
            down = jnp.where(low_lanes, lanes_swapped(edge.reshape(256, LOW)).reshape(32, 8, LOW), inner)
            xs.append(jnp.concatenate([up, down], axis=1).reshape(NZ, LOW))
        xh, xl = halves(jnp.concatenate(xs, axis=1))
        y = dot3(high_ref[...], low_ref[...], xh, xl)
        for k in range(2):
            e = 2 * pair + k
            lanes = slice(LOW * k, LOW * k + LOW)
            u = dot(jnp.concatenate([xh[:, lanes], xl[:, lanes], xh[:, lanes]], axis=1), slope)
            z = y[:, lanes] + u[:, :LOW] * advect_ref[0, pl.ds(e, 1), :] + u[:, LOW:] * advect_ref[1, pl.ds(e, 1), :]
            z = z - xs[k] * count
            out_ref[:, e] = z.reshape(32, 16, LOW)


def stacked3(table, axis):
    high, low = split_table(table)
    return np.concatenate([high, high, low], axis=axis)


def exchange(x):
    return lax.all_to_all(x, "span", split_axis=0, concat_axis=0, tiled=True)


def shifted(block, distance):
    devices = lax.axis_size("mesh")
    return lax.ppermute(block, "mesh", [((i - distance) % devices, i) for i in range(devices)])


def link_tables(send_rows, neighbours):
    elems = neighbours.shape[1]
    capacity = send_rows.shape[2]
    count = lax.axis_size("mesh")
    here = lax.axis_index("mesh")
    before, after = (here - 1) % count, (here + 1) % count

    def lane(v):
        return (v % 4) * elems + v // 4

    def rows(peer):
        chosen = lax.dynamic_index_in_dim(send_rows[0], peer, 0, keepdims=False)
        return jnp.pad(lane(chosen), (0, 32 - capacity))

    picks = jnp.concatenate([rows(after), rows(before)])[:, None]
    links = neighbours.reshape(1, 4 * elems)
    offset = links - 4 * elems
    peer, within = offset // capacity, offset % capacity
    index = jnp.where(
        links < 4 * elems,
        lane(links),
        jnp.where(peer == before, 4 * elems + within, jnp.where(peer == after, 4 * elems + 32 + within, -1)),
    )
    return picks.astype(jnp.int32), index.astype(jnp.int32)


def travelled(out):
    return jnp.concatenate([shifted(out[:32], 1), shifted(out[32:], -1)], axis=0)


def shards(field, coupling, advect, send_rows, neighbours):
    high, low = split_table(filter_table())
    order = order_table()
    slope_a, slope_b, count = lane_tables()
    along_a, along_b = derivative_tables()
    pick_b = np.eye(64)[B_NODES]
    near = np.concatenate(
        [along_a[B_NODES], along_b[B_NODES], -PEN * edge_count()[B_NODES][:, None] * pick_b], axis=0
    )
    bf = lambda t: jnp.asarray(t, jnp.bfloat16)
    high, low = jnp.asarray(high), jnp.asarray(low)

    packed = call(pack_kernel, [((LOW * 24, LOW), jnp.float32)], 2 * 10**8)(field, coupling, bf(order))
    arrived = exchange(packed).reshape(32, 4, 24, LOW)

    picks, links = link_tables(send_rows, neighbours)
    trace, out = pl.pallas_call(
        first_traces_kernel,
        out_shape=[jax.ShapeDtypeStruct((128, 1024), jnp.float32), jax.ShapeDtypeStruct((64, 128), jnp.float32)],
        scratch_shapes=[pltpu.VMEM((2, 1024, LOW), jnp.float32)],
        compiler_params=pltpu.CompilerParams(vmem_limit_bytes=16 * 2**20),
        cost_estimate=pl.CostEstimate(flops=10**9, bytes_accessed=3 * 2**20, transcendentals=0),
    )(field, coupling, picks)
    came = travelled(out)
    gain, add = pl.pallas_call(
        first_local_kernel,
        out_shape=[jax.ShapeDtypeStruct((LOW * 8, LOW), jnp.float32)] * 2,
        scratch_shapes=[pltpu.VMEM((16, 32, 256), jnp.float32)],
        compiler_params=pltpu.CompilerParams(vmem_limit_bytes=16 * 2**20),
        cost_estimate=pl.CostEstimate(flops=3 * 10**9, bytes_accessed=4 * 2**20, transcendentals=0),
    )(
        field, coupling, advect[:, np.array(B_NODES)], trace, came, links,
        jnp.asarray(stacked3(near, 1)), bf(pick_b),
    )

    lanes = advect[:, np.array(B_NODES + I_NODES)].reshape(2, 2, 32, 2, LOW)
    lanes = lanes.transpose(0, 4, 1, 3, 2).reshape(2, LOW, LOW)
    own = lax.dynamic_slice_in_dim(lanes, 4 * lax.axis_index("span"), 4, axis=1)
    own_inner = jnp.concatenate([own[0, :, 64:], own[1, :, 64:]], axis=1)

    edge, inner = call(first_filter_kernel, [((32, 4, 8, LOW), jnp.float32)] * 2, 10**9)(arrived, high, low)
    edge_back = exchange(edge.reshape(LOW * 8, LOW))

    slope_inner = np.concatenate([slope_a[:, 64:], slope_b[:, 64:]], axis=1)
    inner = call(first_inner_kernel, [((32, 4, 8, LOW), jnp.float32)], 5 * 10**8)(
        arrived, inner, jnp.asarray(stacked3(slope_inner, 0)), own_inner
    )

    edge = edge_back * gain + add
    edge_there = exchange(edge).reshape(32, 4, 8, LOW)

    trace, out = call(
        second_traces_kernel, [((128, 1024), jnp.float32), ((64, 128), jnp.float32)], 5 * 10**8
    )(edge, picks)
    came = travelled(out)
    lift = call(second_local_kernel, [((16, 32, 256), jnp.float32)], 10**9)(trace, came, links)

    slope = np.concatenate([slope_a, slope_b], axis=1)
    value = call(second_filter_kernel, [((32, 4, 16, LOW), jnp.float32)], 2 * 10**9)(
        edge_there, inner, high, low, jnp.asarray(stacked3(slope, 0)), own,
        jnp.asarray(PEN * count[None, :], jnp.float32),
    )
    value = exchange(value.reshape(LOW * 16, LOW))
    return call(final_kernel, [((16, 64, 256), jnp.float32)], 2 * 10**8)(value, lift, bf(order.T))


def solution(mesh):
    placed = (
        P("span", None, "mesh"),
        P("span", None, "mesh"),
        P(None, None, "mesh"),
        P("mesh", None, None),
        P(None, "mesh"),
    )
    return jax.shard_map(shards, mesh=mesh, in_specs=placed, out_specs=P("span", None, "mesh"), check_vma=False)
```

```python
import functools

import jax
import jax.numpy as jnp
import numpy as np
from jax import lax
from jax.experimental import pallas as pl
from jax.experimental.pallas import tpu as pltpu
from jax.sharding import PartitionSpec as P


NZ = 512
PLANES = 16
PEN = 0.3
LOW = 128

EDGE_B = (
    [(t, 0) for t in range(8)]
    + [(t, 7) for t in range(8)]
    + [(1, 1)] + [(0, t) for t in range(1, 7)] + [(6, 1)]
    + [(1, 6)] + [(7, t) for t in range(1, 7)] + [(6, 6)]
)
B_NODES = [8 * b + a for a, b in EDGE_B]
I_NODES = [n for n in range(64) if n not in B_NODES]


def split_table(table):
    high = table.astype(jnp.bfloat16)
    low = (table - np.asarray(high, np.float64)).astype(jnp.bfloat16)
    return np.asarray(high), np.asarray(low)


def filter_table():
    wave = np.arange(NZ // 2 + 1)
    keep = np.where(3 * wave <= NZ, 1.0 - 0.5 * (2.0 * wave / NZ) ** 2, 0.0)
    fold = np.where((wave == 0) | (wave == NZ // 2), 1.0, 2.0) / NZ
    lag = np.arange(NZ)
    phase = 2.0 * np.pi * ((wave[:, None] * lag[None, :]) % NZ) / NZ
    row = np.sum((keep * fold)[:, None] * np.cos(phase), axis=0)
    return row[(lag[:, None] - lag[None, :]) % NZ]


def derivative_tables():
    index = np.arange(8)
    points = np.cos(np.pi * index / 7.0)
    weights = np.where((index == 0) | (index == 7), 2.0, 1.0) * (-1.0) ** index
    distance = points[:, None] - points[None, :] + np.eye(8)
    matrix = np.outer(weights, 1.0 / weights) / distance * (1.0 - np.eye(8))
    matrix = matrix - np.eye(8) * np.sum(matrix, axis=1)[:, None]
    return np.kron(np.eye(8), matrix), np.kron(matrix, np.eye(8))


def edge_count():
    count = np.zeros(64)
    for n in range(64):
        a, b = n % 8, n // 8
        count[n] = (a == 0) + (a == 7) + (b == 0) + (b == 7)
    return count


def lane_node(lane):
    which, rest = divmod(lane, 64)
    half, i = divmod(rest, 32)
    return half, (B_NODES if which == 0 else I_NODES)[i]


def order_table():
    table = np.zeros((128, 128))
    for lane in range(128):
        half, node = lane_node(lane)
        table[lane, 64 * half + node] = 1.0
    return table


def lane_tables():
    along_a, along_b = derivative_tables()
    out = [np.zeros((128, 128)) for _ in range(2)]
    for k, matrix in enumerate((along_a, along_b)):
        for p in range(128):
            for n in range(128):
                hp, np_ = lane_node(p)
                hn, nn = lane_node(n)
                if hp == hn:
                    out[k][n, p] = matrix[np_, nn]
    count = np.array([edge_count()[lane_node(p)[1]] for p in range(128)])
    return out[0], out[1], count


def iota(shape, axis):
    return lax.broadcasted_iota(jnp.int32, shape, axis)


def halves(x):
    high = x.astype(jnp.bfloat16)
    return high, (x - high.astype(jnp.float32)).astype(jnp.bfloat16)


def dot(a, b):
    return jnp.dot(a, b, preferred_element_type=jnp.float32)


def dot3(ah, al, bh, bl):
    return dot(ah, bh) + dot(ah, bl) + dot(al, bh)


def stack_halves(x):
    return jnp.concatenate([x[:, :LOW], x[:, LOW:]], axis=0)


def call(kernel, outs, flops, limit=16):
    def run(*args):
        moved = sum(a.size * a.dtype.itemsize for a in args)
        moved += sum(int(np.prod(o[0])) * 4 for o in outs)
        shapes = [jax.ShapeDtypeStruct(o[0], o[1]) for o in outs]
        result = pl.pallas_call(
            kernel,
            out_shape=shapes if len(shapes) > 1 else shapes[0],
            compiler_params=pltpu.CompilerParams(vmem_limit_bytes=limit * 2**20),
            cost_estimate=pl.CostEstimate(flops=flops, bytes_accessed=moved, transcendentals=0),
        )(*args)
        return result

    return run


def pack_kernel(field_ref, coupling_ref, order_ref, out_ref):
    order = order_ref[...]
    inner = order[64:]
    for j in range(PLANES):
        c = coupling_ref[j]
        x = stack_halves(field_ref[j] * (1.0 + c))
        xh, xl = halves(x)
        out_ref[pl.ds(j, LOW, stride=24), :] = (dot(order, xh) + dot(order, xl)).T
    for j in range(8):
        parts = []
        for up in (0, 8):
            ch, cl = halves(stack_halves(coupling_ref[j + up]))
            parts.append(dot(inner, ch) + dot(inner, cl))
        out_ref[pl.ds(16 + j, LOW, stride=24), :] = jnp.concatenate(parts, axis=0).T


def one_hot_rows(index_ref, width):
    index = index_ref[...]
    hot = iota((index.shape[0], width), 1) == index
    return jnp.where(hot, 1.0, 0.0).astype(jnp.bfloat16)


def one_hot_cols(index_ref, first, count):
    index = index_ref[...]
    hot = (iota((count, index.shape[1]), 0) + first) == index
    return jnp.where(hot, 1.0, 0.0).astype(jnp.bfloat16)


NT = (((1,), (1,)), ((), ()))


def dot_nt(a, b):
    return lax.dot_general(a, b, NT, preferred_element_type=jnp.float32)


def sent(trace, pick_ref, sent_ref):
    th, tl = halves(trace)
    pick = one_hot_rows(pick_ref, 1024)
    sent_ref[...] = dot_nt(pick, th) + dot_nt(pick, tl)


def first_traces_kernel(field_ref, coupling_ref, pick_ref, trace_ref, sent_ref, mixed):
    for j in range(PLANES):
        x = field_ref[j] * (1.0 + coupling_ref[j])
        mixed[0, pl.ds(64 * j, 64), :] = x[:, :LOW]
        mixed[1, pl.ds(64 * j, 64), :] = x[:, LOW:]
        trace_ref[pl.ds(8 * j, 8), pl.ds(0, 256)] = x[:8]
        trace_ref[pl.ds(8 * j, 8), pl.ds(512, 256)] = x[56:]
    for h in range(2):
        trace_ref[:, pl.ds(256 + LOW * h, LOW)] = mixed[h, pl.ds(7, 128, stride=8), :]
        trace_ref[:, pl.ds(768 + LOW * h, LOW)] = mixed[h, pl.ds(0, 128, stride=8), :]
    sent(trace_ref[...], pick_ref, sent_ref)


def outer_traces(trace_ref, came_ref, link_ref):
    th, tl = halves(trace_ref[...])
    ch, cl = halves(came_ref[...].T)
    here = one_hot_cols(link_ref, 0, 1024)
    there = one_hot_cols(link_ref, 1024, 64)
    return dot(th, here) + dot(tl, here) + dot(ch, there) + dot(cl, there)


def lifted(outer):
    f0, f1, f2, f3 = (outer[:, 256 * f : 256 * f + 256].reshape(16, 8, 256) for f in range(4))
    t = iota((16, 8, 256), 1)
    first, last = t == 0, t == 7
    g0 = f0 + jnp.where(first, f3[:, 0:1], 0.0) + jnp.where(last, f1[:, 0:1], 0.0)
    g1 = f2 + jnp.where(first, f3[:, 7:8], 0.0) + jnp.where(last, f1[:, 7:8], 0.0)
    ends = first | last
    return g0, g1, jnp.where(ends, 0.0, f3), jnp.where(ends, 0.0, f1)


def first_local_kernel(
    field_ref, coupling_ref, advect_ref, trace_ref, came_ref, link_ref, near_ref, pick_ref, gain_ref, add_ref, lift
):
    for g, part in enumerate(lifted(outer_traces(trace_ref, came_ref, link_ref))):
        lift[:, pl.ds(8 * g, 8), :] = part * PEN
    near = near_ref[...]
    pick = pick_ref[...]
    ad_a, ad_b = advect_ref[0], advect_ref[1]

    def plane(j):
        c = coupling_ref[j]
        xh, xl = halves(field_ref[j] * (1.0 + c))
        parts = dot(near, jnp.concatenate([xh, xl, xh], axis=0))
        ch, cl = halves(c)
        gain = 1.0 + (dot(pick, ch) + dot(pick, cl))
        local = ad_a * parts[0:32] + ad_b * parts[32:64] + parts[64:96] + lift[j]
        return gain, gain * local

    for j in range(8):
        gains, adds = [], []
        for up in (0, 8):
            gain, add = plane(j + up)
            gains.append(stack_halves(gain))
            adds.append(stack_halves(add))
        gain_ref[pl.ds(j, LOW, stride=8), :] = jnp.concatenate(gains, axis=0).T
        add_ref[pl.ds(j, LOW, stride=8), :] = jnp.concatenate(adds, axis=0).T


def second_traces_kernel(value_ref, pick_ref, trace_ref, sent_ref):
    t = iota((8, 256), 0)
    for j in range(8):
        rows = value_ref[pl.ds(j, LOW, stride=8), :].T
        for up in range(2):
            part = rows[64 * up : 64 * up + 64]
            g = [
                jnp.concatenate([part[8 * k : 8 * k + 8], part[32 + 8 * k : 40 + 8 * k]], axis=1) for k in range(4)
            ]
            f3 = jnp.where(t == 0, g[0][0:1], jnp.where(t == 7, g[1][0:1], g[2]))
            f1 = jnp.where(t == 0, g[0][7:8], jnp.where(t == 7, g[1][7:8], g[3]))
            for f, one in enumerate((g[0], f1, g[1], f3)):
                trace_ref[pl.ds(8 * (j + 8 * up), 8), pl.ds(256 * f, 256)] = one
    sent(trace_ref[...], pick_ref, sent_ref)


def second_local_kernel(trace_ref, came_ref, link_ref, lift_ref):
    for g, part in enumerate(lifted(outer_traces(trace_ref, came_ref, link_ref))):
        lift_ref[:, pl.ds(8 * g, 8), :] = part * PEN


def final_kernel(value_ref, lift_ref, back_ref, out_ref):
    back = back_ref[...]
    for j in range(PLANES):
        rows = value_ref[pl.ds(j, LOW, stride=16), :].T
        edge = rows[:64] + stack_halves(lift_ref[j])
        rows = jnp.concatenate([edge, rows[64:]], axis=0)
        rh, rl = halves(rows)
        full = dot(back, rh) + dot(back, rl)
        out_ref[j] = jnp.concatenate([full[:64], full[64:]], axis=1)


def lanes_swapped(x):
    return pltpu.roll(x, 64, x.ndim - 1)


def first_filter_kernel(value_ref, high_ref, low_ref, edge_ref, inner_ref):
    low_lanes = iota((32, 8, LOW), 2) < 64
    for pair in range(2):
        xs = [value_ref[:, 2 * pair + k, pl.ds(0, 16), :].reshape(NZ, LOW) for k in range(2)]
        xh, xl = halves(jnp.concatenate(xs, axis=1))
        y = dot3(high_ref[...], low_ref[...], xh, xl)
        for k in range(2):
            e = 2 * pair + k
            rows = y[:, LOW * k : LOW * k + LOW].reshape(32, 16, LOW)
            up, down = rows[:, :8], rows[:, 8:]
            edge_ref[:, e] = jnp.where(low_lanes, up, lanes_swapped(down.reshape(256, LOW)).reshape(32, 8, LOW))
            inner_ref[:, e] = jnp.where(low_lanes, lanes_swapped(up.reshape(256, LOW)).reshape(32, 8, LOW), down)


def first_inner_kernel(value_ref, inner_ref, slope_ref, advect_ref, out_ref):
    low_lanes = iota((32, 8, LOW), 2) < 64
    slope = slope_ref[...]
    for e in range(4):
        xh, xl = halves(value_ref[:, e, pl.ds(0, 16), :].reshape(NZ, LOW))
        u = dot(jnp.concatenate([xh, xl, xh], axis=1), slope) * advect_ref[pl.ds(e, 1), :]
        v = (u + lanes_swapped(u)).reshape(32, 16, LOW)
        local = jnp.where(low_lanes, v[:, :8], v[:, 8:])
        out_ref[:, e] = (inner_ref[:, e] + local) * (1.0 + value_ref[:, e, pl.ds(16, 8), :])


def second_filter_kernel(edge_ref, inner_ref, high_ref, low_ref, slope_ref, advect_ref, count_ref, out_ref):
    low_lanes = iota((32, 8, LOW), 2) < 64
    slope = slope_ref[...]
    count = count_ref[...]
    for pair in range(2):
        xs = []
        for k in range(2):
            e = 2 * pair + k
            edge, inner = edge_ref[:, e], inner_ref[:, e]
            up = jnp.where(low_lanes, edge, lanes_swapped(inner.reshape(256, LOW)).reshape(32, 8, LOW))
            down = jnp.where(low_lanes, lanes_swapped(edge.reshape(256, LOW)).reshape(32, 8, LOW), inner)
            xs.append(jnp.concatenate([up, down], axis=1).reshape(NZ, LOW))
        xh, xl = halves(jnp.concatenate(xs, axis=1))
        y = dot3(high_ref[...], low_ref[...], xh, xl)
        for k in range(2):
            e = 2 * pair + k
            lanes = slice(LOW * k, LOW * k + LOW)
            u = dot(jnp.concatenate([xh[:, lanes], xl[:, lanes], xh[:, lanes]], axis=1), slope)
            z = y[:, lanes] + u[:, :LOW] * advect_ref[0, pl.ds(e, 1), :] + u[:, LOW:] * advect_ref[1, pl.ds(e, 1), :]
            z = z - xs[k] * count
            out_ref[:, e] = z.reshape(32, 16, LOW)


def stacked3(table, axis):
    high, low = split_table(table)
    return np.concatenate([high, high, low], axis=axis)


def exchange(x):
    return lax.all_to_all(x, "span", split_axis=0, concat_axis=0, tiled=True)


def shifted(block, distance):
    devices = lax.axis_size("mesh")
    return lax.ppermute(block, "mesh", [((i - distance) % devices, i) for i in range(devices)])


def link_tables(send_rows, neighbours):
    elems = neighbours.shape[1]
    capacity = send_rows.shape[2]
    count = lax.axis_size("mesh")
    here = lax.axis_index("mesh")
    before, after = (here - 1) % count, (here + 1) % count

    def lane(v):
        return (v % 4) * elems + v // 4

    def rows(peer):
        chosen = lax.dynamic_index_in_dim(send_rows[0], peer, 0, keepdims=False)
        return jnp.pad(lane(chosen), (0, 32 - capacity))

    picks = jnp.concatenate([rows(after), rows(before)])[:, None]
    links = neighbours.reshape(1, 4 * elems)
    offset = links - 4 * elems
    peer, within = offset // capacity, offset % capacity
    index = jnp.where(
        links < 4 * elems,
        lane(links),
        jnp.where(peer == before, 4 * elems + within, jnp.where(peer == after, 4 * elems + 32 + within, -1)),
    )
    return picks.astype(jnp.int32), index.astype(jnp.int32)


def travelled(out):
    return jnp.concatenate([shifted(out[:32], 1), shifted(out[32:], -1)], axis=0)


def shards(field, coupling, advect, send_rows, neighbours):
    high, low = split_table(filter_table())
    order = order_table()
    slope_a, slope_b, count = lane_tables()
    along_a, along_b = derivative_tables()
    pick_b = np.eye(64)[B_NODES]
    near = np.concatenate(
        [along_a[B_NODES], along_b[B_NODES], -PEN * edge_count()[B_NODES][:, None] * pick_b], axis=0
    )
    bf = lambda t: jnp.asarray(t, jnp.bfloat16)
    high, low = jnp.asarray(high), jnp.asarray(low)

    packed = call(pack_kernel, [((LOW * 24, LOW), jnp.float32)], 2 * 10**8)(field, coupling, bf(order))
    arrived = exchange(packed).reshape(32, 4, 24, LOW)

    picks, links = link_tables(send_rows, neighbours)
    trace, out = pl.pallas_call(
        first_traces_kernel,
        out_shape=[jax.ShapeDtypeStruct((128, 1024), jnp.float32), jax.ShapeDtypeStruct((64, 128), jnp.float32)],
        scratch_shapes=[pltpu.VMEM((2, 1024, LOW), jnp.float32)],
        compiler_params=pltpu.CompilerParams(vmem_limit_bytes=16 * 2**20),
        cost_estimate=pl.CostEstimate(flops=10**9, bytes_accessed=3 * 2**20, transcendentals=0),
    )(field, coupling, picks)
    came = travelled(out)
    gain, add = pl.pallas_call(
        first_local_kernel,
        out_shape=[jax.ShapeDtypeStruct((LOW * 8, LOW), jnp.float32)] * 2,
        scratch_shapes=[pltpu.VMEM((16, 32, 256), jnp.float32)],
        compiler_params=pltpu.CompilerParams(vmem_limit_bytes=16 * 2**20),
        cost_estimate=pl.CostEstimate(flops=3 * 10**9, bytes_accessed=4 * 2**20, transcendentals=0),
    )(
        field, coupling, advect[:, np.array(B_NODES)], trace, came, links,
        jnp.asarray(stacked3(near, 1)), bf(pick_b),
    )

    lanes = advect[:, np.array(B_NODES + I_NODES)].reshape(2, 2, 32, 2, LOW)
    lanes = lanes.transpose(0, 4, 1, 3, 2).reshape(2, LOW, LOW)
    own = lax.dynamic_slice_in_dim(lanes, 4 * lax.axis_index("span"), 4, axis=1)
    own_inner = jnp.concatenate([own[0, :, 64:], own[1, :, 64:]], axis=1)

    edge, inner = call(first_filter_kernel, [((32, 4, 8, LOW), jnp.float32)] * 2, 10**9)(arrived, high, low)
    edge_back = exchange(edge.reshape(LOW * 8, LOW))

    slope_inner = np.concatenate([slope_a[:, 64:], slope_b[:, 64:]], axis=1)
    inner = call(first_inner_kernel, [((32, 4, 8, LOW), jnp.float32)], 5 * 10**8)(
        arrived, inner, jnp.asarray(stacked3(slope_inner, 0)), own_inner
    )

    edge = edge_back * gain + add
    edge_there = exchange(edge).reshape(32, 4, 8, LOW)

    trace, out = call(
        second_traces_kernel, [((128, 1024), jnp.float32), ((64, 128), jnp.float32)], 5 * 10**8
    )(edge, picks)
    came = travelled(out)
    lift = call(second_local_kernel, [((16, 32, 256), jnp.float32)], 10**9)(trace, came, links)

    slope = np.concatenate([slope_a, slope_b], axis=1)
    edge_there, lift = lax.optimization_barrier((edge_there, lift))
    value = call(second_filter_kernel, [((32, 4, 16, LOW), jnp.float32)], 2 * 10**9)(
        edge_there, inner, high, low, jnp.asarray(stacked3(slope, 0)), own,
        jnp.asarray(PEN * count[None, :], jnp.float32),
    )
    value = exchange(value.reshape(LOW * 16, LOW))
    return call(final_kernel, [((16, 64, 256), jnp.float32)], 2 * 10**8)(value, lift, bf(order.T))


def solution(mesh):
    placed = (
        P("span", None, "mesh"),
        P("span", None, "mesh"),
        P(None, None, "mesh"),
        P("mesh", None, None),
        P(None, "mesh"),
    )
    return jax.shard_map(shards, mesh=mesh, in_specs=placed, out_specs=P("span", None, "mesh"), check_vma=False)
```

```python
import functools

import jax
import jax.numpy as jnp
import numpy as np
from jax import lax
from jax.experimental import pallas as pl
from jax.experimental.pallas import tpu as pltpu
from jax.sharding import PartitionSpec as P


NZ = 512
PLANES = 16
PEN = 0.3
LOW = 128

EDGE_B = (
    [(t, 0) for t in range(8)]
    + [(t, 7) for t in range(8)]
    + [(1, 1)] + [(0, t) for t in range(1, 7)] + [(6, 1)]
    + [(1, 6)] + [(7, t) for t in range(1, 7)] + [(6, 6)]
)
B_NODES = [8 * b + a for a, b in EDGE_B]
I_NODES = [n for n in range(64) if n not in B_NODES]


def split_table(table):
    high = table.astype(jnp.bfloat16)
    low = (table - np.asarray(high, np.float64)).astype(jnp.bfloat16)
    return np.asarray(high), np.asarray(low)


def filter_table():
    wave = np.arange(NZ // 2 + 1)
    keep = np.where(3 * wave <= NZ, 1.0 - 0.5 * (2.0 * wave / NZ) ** 2, 0.0)
    fold = np.where((wave == 0) | (wave == NZ // 2), 1.0, 2.0) / NZ
    lag = np.arange(NZ)
    phase = 2.0 * np.pi * ((wave[:, None] * lag[None, :]) % NZ) / NZ
    row = np.sum((keep * fold)[:, None] * np.cos(phase), axis=0)
    return row[(lag[:, None] - lag[None, :]) % NZ]


def derivative_tables():
    index = np.arange(8)
    points = np.cos(np.pi * index / 7.0)
    weights = np.where((index == 0) | (index == 7), 2.0, 1.0) * (-1.0) ** index
    distance = points[:, None] - points[None, :] + np.eye(8)
    matrix = np.outer(weights, 1.0 / weights) / distance * (1.0 - np.eye(8))
    matrix = matrix - np.eye(8) * np.sum(matrix, axis=1)[:, None]
    return np.kron(np.eye(8), matrix), np.kron(matrix, np.eye(8))


def edge_count():
    count = np.zeros(64)
    for n in range(64):
        a, b = n % 8, n // 8
        count[n] = (a == 0) + (a == 7) + (b == 0) + (b == 7)
    return count


def lane_node(lane):
    which, rest = divmod(lane, 64)
    half, i = divmod(rest, 32)
    return half, (B_NODES if which == 0 else I_NODES)[i]


def order_table():
    table = np.zeros((128, 128))
    for lane in range(128):
        half, node = lane_node(lane)
        table[lane, 64 * half + node] = 1.0
    return table


def lane_tables():
    along_a, along_b = derivative_tables()
    out = [np.zeros((128, 128)) for _ in range(2)]
    for k, matrix in enumerate((along_a, along_b)):
        for p in range(128):
            for n in range(128):
                hp, np_ = lane_node(p)
                hn, nn = lane_node(n)
                if hp == hn:
                    out[k][n, p] = matrix[np_, nn]
    count = np.array([edge_count()[lane_node(p)[1]] for p in range(128)])
    return out[0], out[1], count


def iota(shape, axis):
    return lax.broadcasted_iota(jnp.int32, shape, axis)


def halves(x):
    high = x.astype(jnp.bfloat16)
    return high, (x - high.astype(jnp.float32)).astype(jnp.bfloat16)


def dot(a, b):
    return jnp.dot(a, b, preferred_element_type=jnp.float32)


def dot3(ah, al, bh, bl):
    return dot(ah, bh) + dot(ah, bl) + dot(al, bh)


def stack_halves(x):
    return jnp.concatenate([x[:, :LOW], x[:, LOW:]], axis=0)


def call(kernel, outs, flops, limit=16):
    def run(*args):
        moved = sum(a.size * a.dtype.itemsize for a in args)
        moved += sum(int(np.prod(o[0])) * 4 for o in outs)
        shapes = [jax.ShapeDtypeStruct(o[0], o[1]) for o in outs]
        result = pl.pallas_call(
            kernel,
            out_shape=shapes if len(shapes) > 1 else shapes[0],
            compiler_params=pltpu.CompilerParams(vmem_limit_bytes=limit * 2**20),
            cost_estimate=pl.CostEstimate(flops=flops, bytes_accessed=moved, transcendentals=0),
        )(*args)
        return result

    return run


def pack_kernel(field_ref, coupling_ref, order_ref, out_ref):
    order = order_ref[...]
    inner = order[64:]
    for j in range(PLANES):
        c = coupling_ref[j]
        x = stack_halves(field_ref[j] * (1.0 + c))
        xh, xl = halves(x)
        out_ref[pl.ds(j, LOW, stride=24), :] = (dot(order, xh) + dot(order, xl)).T
    for j in range(8):
        parts = []
        for up in (0, 8):
            ch, cl = halves(stack_halves(coupling_ref[j + up]))
            parts.append(dot(inner, ch) + dot(inner, cl))
        out_ref[pl.ds(16 + j, LOW, stride=24), :] = jnp.concatenate(parts, axis=0).T


def one_hot_rows(index_ref, width):
    index = index_ref[...]
    hot = iota((index.shape[0], width), 1) == index
    return jnp.where(hot, 1.0, 0.0).astype(jnp.bfloat16)


def one_hot_cols(index_ref, first, count):
    index = index_ref[...]
    hot = (iota((count, index.shape[1]), 0) + first) == index
    return jnp.where(hot, 1.0, 0.0).astype(jnp.bfloat16)


NT = (((1,), (1,)), ((), ()))


def dot_nt(a, b):
    return lax.dot_general(a, b, NT, preferred_element_type=jnp.float32)


def sent(trace, pick_ref, sent_ref):
    th, tl = halves(trace)
    pick = one_hot_rows(pick_ref, 1024)
    sent_ref[...] = dot_nt(pick, th) + dot_nt(pick, tl)


def first_traces_kernel(field_ref, coupling_ref, pick_ref, trace_ref, sent_ref, mixed):
    for j in range(PLANES):
        x = field_ref[j] * (1.0 + coupling_ref[j])
        mixed[0, pl.ds(64 * j, 64), :] = x[:, :LOW]
        mixed[1, pl.ds(64 * j, 64), :] = x[:, LOW:]
        trace_ref[pl.ds(8 * j, 8), pl.ds(0, 256)] = x[:8]
        trace_ref[pl.ds(8 * j, 8), pl.ds(512, 256)] = x[56:]
    for h in range(2):
        trace_ref[:, pl.ds(256 + LOW * h, LOW)] = mixed[h, pl.ds(7, 128, stride=8), :]
        trace_ref[:, pl.ds(768 + LOW * h, LOW)] = mixed[h, pl.ds(0, 128, stride=8), :]
    sent(trace_ref[...], pick_ref, sent_ref)


def outer_traces(trace_ref, came_ref, link_ref):
    th, tl = halves(trace_ref[...])
    ch, cl = halves(came_ref[...].T)
    here = one_hot_cols(link_ref, 0, 1024)
    there = one_hot_cols(link_ref, 1024, 64)
    return dot(th, here) + dot(tl, here) + dot(ch, there) + dot(cl, there)


def lifted(outer):
    f0, f1, f2, f3 = (outer[:, 256 * f : 256 * f + 256].reshape(16, 8, 256) for f in range(4))
    t = iota((16, 8, 256), 1)
    first, last = t == 0, t == 7
    g0 = f0 + jnp.where(first, f3[:, 0:1], 0.0) + jnp.where(last, f1[:, 0:1], 0.0)
    g1 = f2 + jnp.where(first, f3[:, 7:8], 0.0) + jnp.where(last, f1[:, 7:8], 0.0)
    ends = first | last
    return g0, g1, jnp.where(ends, 0.0, f3), jnp.where(ends, 0.0, f1)


def first_local_kernel(
    field_ref, coupling_ref, advect_ref, trace_ref, came_ref, link_ref, near_ref, pick_ref, gain_ref, add_ref, lift
):
    for g, part in enumerate(lifted(outer_traces(trace_ref, came_ref, link_ref))):
        lift[:, pl.ds(8 * g, 8), :] = part * PEN
    near = near_ref[...]
    pick = pick_ref[...]
    ad_a, ad_b = advect_ref[0], advect_ref[1]

    def plane(j):
        c = coupling_ref[j]
        xh, xl = halves(field_ref[j] * (1.0 + c))
        parts = dot(near, jnp.concatenate([xh, xl, xh], axis=0))
        ch, cl = halves(c)
        gain = 1.0 + (dot(pick, ch) + dot(pick, cl))
        local = ad_a * parts[0:32] + ad_b * parts[32:64] + parts[64:96] + lift[j]
        return gain, gain * local

    for j in range(8):
        gains, adds = [], []
        for up in (0, 8):
            gain, add = plane(j + up)
            gains.append(stack_halves(gain))
            adds.append(stack_halves(add))
        gain_ref[pl.ds(j, LOW, stride=8), :] = jnp.concatenate(gains, axis=0).T
        add_ref[pl.ds(j, LOW, stride=8), :] = jnp.concatenate(adds, axis=0).T


def second_traces_kernel(value_ref, pick_ref, trace_ref, sent_ref):
    t = iota((8, 256), 0)
    for j in range(8):
        rows = value_ref[pl.ds(j, LOW, stride=8), :].T
        for up in range(2):
            part = rows[64 * up : 64 * up + 64]
            g = [
                jnp.concatenate([part[8 * k : 8 * k + 8], part[32 + 8 * k : 40 + 8 * k]], axis=1) for k in range(4)
            ]
            f3 = jnp.where(t == 0, g[0][0:1], jnp.where(t == 7, g[1][0:1], g[2]))
            f1 = jnp.where(t == 0, g[0][7:8], jnp.where(t == 7, g[1][7:8], g[3]))
            for f, one in enumerate((g[0], f1, g[1], f3)):
                trace_ref[pl.ds(8 * (j + 8 * up), 8), pl.ds(256 * f, 256)] = one
    sent(trace_ref[...], pick_ref, sent_ref)


def second_local_kernel(trace_ref, came_ref, link_ref, lift_ref):
    for g, part in enumerate(lifted(outer_traces(trace_ref, came_ref, link_ref))):
        lift_ref[:, pl.ds(8 * g, 8), :] = part * PEN


def final_kernel(value_ref, lift_ref, back_ref, out_ref):
    back = back_ref[...]
    for j in range(PLANES):
        rows = value_ref[pl.ds(j, LOW, stride=16), :].T
        edge = rows[:64] + stack_halves(lift_ref[j])
        rows = jnp.concatenate([edge, rows[64:]], axis=0)
        rh, rl = halves(rows)
        full = dot(back, rh) + dot(back, rl)
        out_ref[j] = jnp.concatenate([full[:64], full[64:]], axis=1)


def lanes_swapped(x):
    return pltpu.roll(x, 64, x.ndim - 1)


def first_filter_kernel(value_ref, high_ref, low_ref, edge_ref, inner_ref):
    low_lanes = iota((32, 8, LOW), 2) < 64
    for pair in range(2):
        xs = [value_ref[:, 2 * pair + k, pl.ds(0, 16), :].reshape(NZ, LOW) for k in range(2)]
        xh, xl = halves(jnp.concatenate(xs, axis=1))
        y = dot3(high_ref[...], low_ref[...], xh, xl)
        for k in range(2):
            e = 2 * pair + k
            rows = y[:, LOW * k : LOW * k + LOW].reshape(32, 16, LOW)
            up, down = rows[:, :8], rows[:, 8:]
            edge_ref[:, e] = jnp.where(low_lanes, up, lanes_swapped(down.reshape(256, LOW)).reshape(32, 8, LOW))
            inner_ref[:, e] = jnp.where(low_lanes, lanes_swapped(up.reshape(256, LOW)).reshape(32, 8, LOW), down)


def first_inner_kernel(value_ref, inner_ref, slope_ref, advect_ref, out_ref):
    low_lanes = iota((32, 8, LOW), 2) < 64
    slope = slope_ref[...]
    for e in range(4):
        xh, xl = halves(value_ref[:, e, pl.ds(0, 16), :].reshape(NZ, LOW))
        u = dot(jnp.concatenate([xh, xl, xh], axis=1), slope) * advect_ref[pl.ds(e, 1), :]
        v = (u + lanes_swapped(u)).reshape(32, 16, LOW)
        local = jnp.where(low_lanes, v[:, :8], v[:, 8:])
        out_ref[:, e] = (inner_ref[:, e] + local) * (1.0 + value_ref[:, e, pl.ds(16, 8), :])


def combine_kernel(value_ref, gain_ref, add_ref, out_ref):
    out_ref[...] = value_ref[...] * gain_ref[...] + add_ref[...]


def second_filter_kernel(edge_ref, inner_ref, high_ref, low_ref, slope_ref, advect_ref, count_ref, out_ref):
    low_lanes = iota((32, 8, LOW), 2) < 64
    slope = slope_ref[...]
    count = count_ref[...]
    for pair in range(2):
        xs = []
        for k in range(2):
            e = 2 * pair + k
            edge, inner = edge_ref[:, e], inner_ref[:, e]
            up = jnp.where(low_lanes, edge, lanes_swapped(inner.reshape(256, LOW)).reshape(32, 8, LOW))
            down = jnp.where(low_lanes, lanes_swapped(edge.reshape(256, LOW)).reshape(32, 8, LOW), inner)
            xs.append(jnp.concatenate([up, down], axis=1).reshape(NZ, LOW))
        xh, xl = halves(jnp.concatenate(xs, axis=1))
        y = dot3(high_ref[...], low_ref[...], xh, xl)
        for k in range(2):
            e = 2 * pair + k
            lanes = slice(LOW * k, LOW * k + LOW)
            u = dot(jnp.concatenate([xh[:, lanes], xl[:, lanes], xh[:, lanes]], axis=1), slope)
            z = y[:, lanes] + u[:, :LOW] * advect_ref[0, pl.ds(e, 1), :] + u[:, LOW:] * advect_ref[1, pl.ds(e, 1), :]
            z = z - xs[k] * count
            out_ref[:, e] = z.reshape(32, 16, LOW)


def stacked3(table, axis):
    high, low = split_table(table)
    return np.concatenate([high, high, low], axis=axis)


def exchange(x):
    return lax.all_to_all(x, "span", split_axis=0, concat_axis=0, tiled=True)


def shifted(block, distance):
    devices = lax.axis_size("mesh")
    return lax.ppermute(block, "mesh", [((i - distance) % devices, i) for i in range(devices)])


def link_tables(send_rows, neighbours):
    elems = neighbours.shape[1]
    capacity = send_rows.shape[2]
    count = lax.axis_size("mesh")
    here = lax.axis_index("mesh")
    before, after = (here - 1) % count, (here + 1) % count

    def lane(v):
        return (v % 4) * elems + v // 4

    def rows(peer):
        chosen = lax.dynamic_index_in_dim(send_rows[0], peer, 0, keepdims=False)
        return jnp.pad(lane(chosen), (0, 32 - capacity))

    picks = jnp.concatenate([rows(after), rows(before)])[:, None]
    links = neighbours.reshape(1, 4 * elems)
    offset = links - 4 * elems
    peer, within = offset // capacity, offset % capacity
    index = jnp.where(
        links < 4 * elems,
        lane(links),
        jnp.where(peer == before, 4 * elems + within, jnp.where(peer == after, 4 * elems + 32 + within, -1)),
    )
    return picks.astype(jnp.int32), index.astype(jnp.int32)


def travelled(out):
    return jnp.concatenate([shifted(out[:32], 1), shifted(out[32:], -1)], axis=0)


def shards(field, coupling, advect, send_rows, neighbours):
    high, low = split_table(filter_table())
    order = order_table()
    slope_a, slope_b, count = lane_tables()
    along_a, along_b = derivative_tables()
    pick_b = np.eye(64)[B_NODES]
    near = np.concatenate(
        [along_a[B_NODES], along_b[B_NODES], -PEN * edge_count()[B_NODES][:, None] * pick_b], axis=0
    )
    bf = lambda t: jnp.asarray(t, jnp.bfloat16)
    high, low = jnp.asarray(high), jnp.asarray(low)

    packed = call(pack_kernel, [((LOW * 24, LOW), jnp.float32)], 2 * 10**8, 60)(field, coupling, bf(order))
    arrived = exchange(packed).reshape(32, 4, 24, LOW)

    picks, links = link_tables(send_rows, neighbours)
    trace, out = pl.pallas_call(
        first_traces_kernel,
        out_shape=[jax.ShapeDtypeStruct((128, 1024), jnp.float32), jax.ShapeDtypeStruct((64, 128), jnp.float32)],
        scratch_shapes=[pltpu.VMEM((2, 1024, LOW), jnp.float32)],
        compiler_params=pltpu.CompilerParams(vmem_limit_bytes=16 * 2**20),
        cost_estimate=pl.CostEstimate(flops=10**9, bytes_accessed=3 * 2**20, transcendentals=0),
    )(field, coupling, picks)
    came = travelled(out)
    gain, add = pl.pallas_call(
        first_local_kernel,
        out_shape=[jax.ShapeDtypeStruct((LOW * 8, LOW), jnp.float32)] * 2,
        scratch_shapes=[pltpu.VMEM((16, 32, 256), jnp.float32)],
        compiler_params=pltpu.CompilerParams(vmem_limit_bytes=16 * 2**20),
        cost_estimate=pl.CostEstimate(flops=3 * 10**9, bytes_accessed=4 * 2**20, transcendentals=0),
    )(
        field, coupling, advect[:, np.array(B_NODES)], trace, came, links,
        jnp.asarray(stacked3(near, 1)), bf(pick_b),
    )

    lanes = advect[:, np.array(B_NODES + I_NODES)].reshape(2, 2, 32, 2, LOW)
    lanes = lanes.transpose(0, 4, 1, 3, 2).reshape(2, LOW, LOW)
    own = lax.dynamic_slice_in_dim(lanes, 4 * lax.axis_index("span"), 4, axis=1)
    own_inner = jnp.concatenate([own[0, :, 64:], own[1, :, 64:]], axis=1)

    edge, inner = call(first_filter_kernel, [((32, 4, 8, LOW), jnp.float32)] * 2, 10**9)(arrived, high, low)
    edge_back = exchange(edge.reshape(LOW * 8, LOW))

    slope_inner = np.concatenate([slope_a[:, 64:], slope_b[:, 64:]], axis=1)
    inner = call(first_inner_kernel, [((32, 4, 8, LOW), jnp.float32)], 5 * 10**8)(
        arrived, inner, jnp.asarray(stacked3(slope_inner, 0)), own_inner
    )

    edge = call(combine_kernel, [((LOW * 8, LOW), jnp.float32)], 10**6, 60)(edge_back, gain, add)
    edge_there = exchange(edge).reshape(32, 4, 8, LOW)

    trace, out = call(
        second_traces_kernel, [((128, 1024), jnp.float32), ((64, 128), jnp.float32)], 5 * 10**8
    )(edge, picks)
    came = travelled(out)
    lift = call(second_local_kernel, [((16, 32, 256), jnp.float32)], 10**9)(trace, came, links)

    slope = np.concatenate([slope_a, slope_b], axis=1)
    edge_there, lift = lax.optimization_barrier((edge_there, lift))
    value = call(second_filter_kernel, [((32, 4, 16, LOW), jnp.float32)], 2 * 10**9)(
        edge_there, inner, high, low, jnp.asarray(stacked3(slope, 0)), own,
        jnp.asarray(PEN * count[None, :], jnp.float32),
    )
    value = exchange(value.reshape(LOW * 16, LOW))
    return call(final_kernel, [((16, 64, 256), jnp.float32)], 2 * 10**8)(value, lift, bf(order.T))


def solution(mesh):
    placed = (
        P("span", None, "mesh"),
        P("span", None, "mesh"),
        P(None, None, "mesh"),
        P("mesh", None, None),
        P(None, "mesh"),
    )
    return jax.shard_map(shards, mesh=mesh, in_specs=placed, out_specs=P("span", None, "mesh"), check_vma=False)
```

```python
import functools

import jax
import jax.numpy as jnp
import numpy as np
from jax import lax
from jax.experimental import pallas as pl
from jax.experimental.pallas import tpu as pltpu
from jax.sharding import PartitionSpec as P


NZ = 512
PLANES = 16
PEN = 0.3
LOW = 128

EDGE_B = (
    [(t, 0) for t in range(8)]
    + [(t, 7) for t in range(8)]
    + [(1, 1)] + [(0, t) for t in range(1, 7)] + [(6, 1)]
    + [(1, 6)] + [(7, t) for t in range(1, 7)] + [(6, 6)]
)
B_NODES = [8 * b + a for a, b in EDGE_B]
I_NODES = [n for n in range(64) if n not in B_NODES]


def split_table(table):
    high = table.astype(jnp.bfloat16)
    low = (table - np.asarray(high, np.float64)).astype(jnp.bfloat16)
    return np.asarray(high), np.asarray(low)


def filter_table():
    wave = np.arange(NZ // 2 + 1)
    keep = np.where(3 * wave <= NZ, 1.0 - 0.5 * (2.0 * wave / NZ) ** 2, 0.0)
    fold = np.where((wave == 0) | (wave == NZ // 2), 1.0, 2.0) / NZ
    lag = np.arange(NZ)
    phase = 2.0 * np.pi * ((wave[:, None] * lag[None, :]) % NZ) / NZ
    row = np.sum((keep * fold)[:, None] * np.cos(phase), axis=0)
    return row[(lag[:, None] - lag[None, :]) % NZ]


def derivative_tables():
    index = np.arange(8)
    points = np.cos(np.pi * index / 7.0)
    weights = np.where((index == 0) | (index == 7), 2.0, 1.0) * (-1.0) ** index
    distance = points[:, None] - points[None, :] + np.eye(8)
    matrix = np.outer(weights, 1.0 / weights) / distance * (1.0 - np.eye(8))
    matrix = matrix - np.eye(8) * np.sum(matrix, axis=1)[:, None]
    return np.kron(np.eye(8), matrix), np.kron(matrix, np.eye(8))


def edge_count():
    count = np.zeros(64)
    for n in range(64):
        a, b = n % 8, n // 8
        count[n] = (a == 0) + (a == 7) + (b == 0) + (b == 7)
    return count


def lane_node(lane):
    which, rest = divmod(lane, 64)
    half, i = divmod(rest, 32)
    return half, (B_NODES if which == 0 else I_NODES)[i]


def order_table():
    table = np.zeros((128, 128))
    for lane in range(128):
        half, node = lane_node(lane)
        table[lane, 64 * half + node] = 1.0
    return table


def lane_tables():
    along_a, along_b = derivative_tables()
    out = [np.zeros((128, 128)) for _ in range(2)]
    for k, matrix in enumerate((along_a, along_b)):
        for p in range(128):
            for n in range(128):
                hp, np_ = lane_node(p)
                hn, nn = lane_node(n)
                if hp == hn:
                    out[k][n, p] = matrix[np_, nn]
    count = np.array([edge_count()[lane_node(p)[1]] for p in range(128)])
    return out[0], out[1], count


def iota(shape, axis):
    return lax.broadcasted_iota(jnp.int32, shape, axis)


def halves(x):
    high = x.astype(jnp.bfloat16)
    return high, (x - high.astype(jnp.float32)).astype(jnp.bfloat16)


def dot(a, b):
    return jnp.dot(a, b, preferred_element_type=jnp.float32)


def dot3(ah, al, bh, bl):
    return dot(ah, bh) + dot(ah, bl) + dot(al, bh)


def stack_halves(x):
    return jnp.concatenate([x[:, :LOW], x[:, LOW:]], axis=0)


def call(kernel, outs, flops, limit=16):
    def run(*args):
        moved = sum(a.size * a.dtype.itemsize for a in args)
        moved += sum(int(np.prod(o[0])) * 4 for o in outs)
        shapes = [jax.ShapeDtypeStruct(o[0], o[1]) for o in outs]
        result = pl.pallas_call(
            kernel,
            out_shape=shapes if len(shapes) > 1 else shapes[0],
            compiler_params=pltpu.CompilerParams(vmem_limit_bytes=limit * 2**20),
            cost_estimate=pl.CostEstimate(flops=flops, bytes_accessed=moved, transcendentals=0),
        )(*args)
        return result

    return run


def pack_kernel(field_ref, coupling_ref, order_ref, out_ref):
    order = order_ref[...]
    inner = order[64:]
    for j in range(PLANES):
        c = coupling_ref[j]
        x = stack_halves(field_ref[j] * (1.0 + c))
        xh, xl = halves(x)
        out_ref[pl.ds(j, LOW, stride=24), :] = (dot(order, xh) + dot(order, xl)).T
    for j in range(8):
        parts = []
        for up in (0, 8):
            ch, cl = halves(stack_halves(coupling_ref[j + up]))
            parts.append(dot(inner, ch) + dot(inner, cl))
        out_ref[pl.ds(16 + j, LOW, stride=24), :] = jnp.concatenate(parts, axis=0).T


def one_hot_rows(index_ref, width):
    index = index_ref[...]
    hot = iota((index.shape[0], width), 1) == index
    return jnp.where(hot, 1.0, 0.0).astype(jnp.bfloat16)


def one_hot_cols(index_ref, first, count):
    index = index_ref[...]
    hot = (iota((count, index.shape[1]), 0) + first) == index
    return jnp.where(hot, 1.0, 0.0).astype(jnp.bfloat16)


NT = (((1,), (1,)), ((), ()))


def dot_nt(a, b):
    return lax.dot_general(a, b, NT, preferred_element_type=jnp.float32)


def sent(trace, pick_ref, sent_ref):
    th, tl = halves(trace)
    pick = one_hot_rows(pick_ref, 1024)
    sent_ref[...] = dot_nt(pick, th) + dot_nt(pick, tl)


def first_traces_kernel(field_ref, coupling_ref, pick_ref, trace_ref, sent_ref, mixed):
    for j in range(PLANES):
        x = field_ref[j] * (1.0 + coupling_ref[j])
        mixed[0, pl.ds(64 * j, 64), :] = x[:, :LOW]
        mixed[1, pl.ds(64 * j, 64), :] = x[:, LOW:]
        trace_ref[pl.ds(8 * j, 8), pl.ds(0, 256)] = x[:8]
        trace_ref[pl.ds(8 * j, 8), pl.ds(512, 256)] = x[56:]
    for h in range(2):
        trace_ref[:, pl.ds(256 + LOW * h, LOW)] = mixed[h, pl.ds(7, 128, stride=8), :]
        trace_ref[:, pl.ds(768 + LOW * h, LOW)] = mixed[h, pl.ds(0, 128, stride=8), :]
    sent(trace_ref[...], pick_ref, sent_ref)


def outer_traces(trace_ref, came_ref, link_ref):
    th, tl = halves(trace_ref[...])
    ch, cl = halves(came_ref[...].T)
    here = one_hot_cols(link_ref, 0, 1024)
    there = one_hot_cols(link_ref, 1024, 64)
    return dot(th, here) + dot(tl, here) + dot(ch, there) + dot(cl, there)


def lifted(outer):
    f0, f1, f2, f3 = (outer[:, 256 * f : 256 * f + 256].reshape(16, 8, 256) for f in range(4))
    t = iota((16, 8, 256), 1)
    first, last = t == 0, t == 7
    g0 = f0 + jnp.where(first, f3[:, 0:1], 0.0) + jnp.where(last, f1[:, 0:1], 0.0)
    g1 = f2 + jnp.where(first, f3[:, 7:8], 0.0) + jnp.where(last, f1[:, 7:8], 0.0)
    ends = first | last
    return g0, g1, jnp.where(ends, 0.0, f3), jnp.where(ends, 0.0, f1)


def first_local_kernel(
    field_ref, coupling_ref, advect_ref, trace_ref, came_ref, link_ref, near_ref, pick_ref, gain_ref, add_ref, lift
):
    for g, part in enumerate(lifted(outer_traces(trace_ref, came_ref, link_ref))):
        lift[:, pl.ds(8 * g, 8), :] = part * PEN
    near = near_ref[...]
    pick = pick_ref[...]
    ad_a, ad_b = advect_ref[0], advect_ref[1]

    def plane(j):
        c = coupling_ref[j]
        xh, xl = halves(field_ref[j] * (1.0 + c))
        parts = dot(near, jnp.concatenate([xh, xl, xh], axis=0))
        ch, cl = halves(c)
        gain = 1.0 + (dot(pick, ch) + dot(pick, cl))
        local = ad_a * parts[0:32] + ad_b * parts[32:64] + parts[64:96] + lift[j]
        return gain, gain * local

    for j in range(8):
        gains, adds = [], []
        for up in (0, 8):
            gain, add = plane(j + up)
            gains.append(stack_halves(gain))
            adds.append(stack_halves(add))
        gain_ref[pl.ds(j, LOW, stride=8), :] = jnp.concatenate(gains, axis=0).T
        add_ref[pl.ds(j, LOW, stride=8), :] = jnp.concatenate(adds, axis=0).T


def second_traces_kernel(value_ref, pick_ref, trace_ref, sent_ref):
    t = iota((8, 256), 0)
    for j in range(8):
        rows = value_ref[pl.ds(j, LOW, stride=8), :].T
        for up in range(2):
            part = rows[64 * up : 64 * up + 64]
            g = [
                jnp.concatenate([part[8 * k : 8 * k + 8], part[32 + 8 * k : 40 + 8 * k]], axis=1) for k in range(4)
            ]
            f3 = jnp.where(t == 0, g[0][0:1], jnp.where(t == 7, g[1][0:1], g[2]))
            f1 = jnp.where(t == 0, g[0][7:8], jnp.where(t == 7, g[1][7:8], g[3]))
            for f, one in enumerate((g[0], f1, g[1], f3)):
                trace_ref[pl.ds(8 * (j + 8 * up), 8), pl.ds(256 * f, 256)] = one
    sent(trace_ref[...], pick_ref, sent_ref)


def second_local_kernel(trace_ref, came_ref, link_ref, lift_ref):
    for g, part in enumerate(lifted(outer_traces(trace_ref, came_ref, link_ref))):
        lift_ref[:, pl.ds(8 * g, 8), :] = part * PEN


def final_kernel(value_ref, lift_ref, back_ref, out_ref):
    back = back_ref[...]
    for j in range(PLANES):
        rows = value_ref[pl.ds(j, LOW, stride=16), :].T
        edge = rows[:64] + stack_halves(lift_ref[j])
        rows = jnp.concatenate([edge, rows[64:]], axis=0)
        rh, rl = halves(rows)
        full = dot(back, rh) + dot(back, rl)
        out_ref[j] = jnp.concatenate([full[:64], full[64:]], axis=1)


def lanes_swapped(x):
    return pltpu.roll(x, 64, x.ndim - 1)


def first_filter_kernel(value_ref, high_ref, low_ref, edge_ref, inner_ref):
    low_lanes = iota((32, 8, LOW), 2) < 64
    for pair in range(2):
        xs = [value_ref[:, 2 * pair + k, pl.ds(0, 16), :].reshape(NZ, LOW) for k in range(2)]
        xh, xl = halves(jnp.concatenate(xs, axis=1))
        y = dot3(high_ref[...], low_ref[...], xh, xl)
        for k in range(2):
            e = 2 * pair + k
            rows = y[:, LOW * k : LOW * k + LOW].reshape(32, 16, LOW)
            up, down = rows[:, :8], rows[:, 8:]
            edge_ref[:, e] = jnp.where(low_lanes, up, lanes_swapped(down.reshape(256, LOW)).reshape(32, 8, LOW))
            inner_ref[:, e] = jnp.where(low_lanes, lanes_swapped(up.reshape(256, LOW)).reshape(32, 8, LOW), down)


def first_inner_kernel(value_ref, inner_ref, slope_ref, advect_ref, out_ref):
    low_lanes = iota((32, 8, LOW), 2) < 64
    slope = slope_ref[...]
    for e in range(4):
        xh, xl = halves(value_ref[:, e, pl.ds(0, 16), :].reshape(NZ, LOW))
        u = dot(jnp.concatenate([xh, xl, xh], axis=1), slope) * advect_ref[pl.ds(e, 1), :]
        v = (u + lanes_swapped(u)).reshape(32, 16, LOW)
        local = jnp.where(low_lanes, v[:, :8], v[:, 8:])
        out_ref[:, e] = (inner_ref[:, e] + local) * (1.0 + value_ref[:, e, pl.ds(16, 8), :])


def second_filter_kernel(edge_ref, inner_ref, high_ref, low_ref, slope_ref, advect_ref, count_ref, out_ref):
    low_lanes = iota((32, 8, LOW), 2) < 64
    slope = slope_ref[...]
    count = count_ref[...]
    for pair in range(2):
        xs = []
        for k in range(2):
            e = 2 * pair + k
            edge, inner = edge_ref[:, e], inner_ref[:, e]
            up = jnp.where(low_lanes, edge, lanes_swapped(inner.reshape(256, LOW)).reshape(32, 8, LOW))
            down = jnp.where(low_lanes, lanes_swapped(edge.reshape(256, LOW)).reshape(32, 8, LOW), inner)
            xs.append(jnp.concatenate([up, down], axis=1).reshape(NZ, LOW))
        xh, xl = halves(jnp.concatenate(xs, axis=1))
        y = dot3(high_ref[...], low_ref[...], xh, xl)
        for k in range(2):
            e = 2 * pair + k
            lanes = slice(LOW * k, LOW * k + LOW)
            u = dot(jnp.concatenate([xh[:, lanes], xl[:, lanes], xh[:, lanes]], axis=1), slope)
            z = y[:, lanes] + u[:, :LOW] * advect_ref[0, pl.ds(e, 1), :] + u[:, LOW:] * advect_ref[1, pl.ds(e, 1), :]
            z = z - xs[k] * count
            out_ref[:, e] = z.reshape(32, 16, LOW)


def stacked3(table, axis):
    high, low = split_table(table)
    return np.concatenate([high, high, low], axis=axis)


def exchange(x):
    return lax.all_to_all(x, "span", split_axis=0, concat_axis=0, tiled=True)


def shifted(block, distance):
    devices = lax.axis_size("mesh")
    return lax.ppermute(block, "mesh", [((i - distance) % devices, i) for i in range(devices)])


def link_tables(send_rows, neighbours):
    elems = neighbours.shape[1]
    capacity = send_rows.shape[2]
    count = lax.axis_size("mesh")
    here = lax.axis_index("mesh")
    before, after = (here - 1) % count, (here + 1) % count

    def lane(v):
        return (v % 4) * elems + v // 4

    def rows(peer):
        chosen = lax.dynamic_index_in_dim(send_rows[0], peer, 0, keepdims=False)
        return jnp.pad(lane(chosen), (0, 32 - capacity))

    picks = jnp.concatenate([rows(after), rows(before)])[:, None]
    links = neighbours.reshape(1, 4 * elems)
    offset = links - 4 * elems
    peer, within = offset // capacity, offset % capacity
    index = jnp.where(
        links < 4 * elems,
        lane(links),
        jnp.where(peer == before, 4 * elems + within, jnp.where(peer == after, 4 * elems + 32 + within, -1)),
    )
    return picks.astype(jnp.int32), index.astype(jnp.int32)


def travelled(out):
    return jnp.concatenate([shifted(out[:32], 1), shifted(out[32:], -1)], axis=0)


def shards(field, coupling, advect, send_rows, neighbours):
    high, low = split_table(filter_table())
    order = order_table()
    slope_a, slope_b, count = lane_tables()
    along_a, along_b = derivative_tables()
    pick_b = np.eye(64)[B_NODES]
    near = np.concatenate(
        [along_a[B_NODES], along_b[B_NODES], -PEN * edge_count()[B_NODES][:, None] * pick_b], axis=0
    )
    bf = lambda t: jnp.asarray(t, jnp.bfloat16)
    high, low = jnp.asarray(high), jnp.asarray(low)

    packed = call(pack_kernel, [((LOW * 24, LOW), jnp.float32)], 2 * 10**8)(field, coupling, bf(order))
    arrived = exchange(packed).reshape(32, 4, 24, LOW)

    picks, links = link_tables(send_rows, neighbours)
    trace, out = pl.pallas_call(
        first_traces_kernel,
        out_shape=[jax.ShapeDtypeStruct((128, 1024), jnp.float32), jax.ShapeDtypeStruct((64, 128), jnp.float32)],
        scratch_shapes=[pltpu.VMEM((2, 1024, LOW), jnp.float32)],
        compiler_params=pltpu.CompilerParams(vmem_limit_bytes=16 * 2**20),
        cost_estimate=pl.CostEstimate(flops=10**9, bytes_accessed=3 * 2**20, transcendentals=0),
    )(field, coupling, picks)
    came = travelled(out)
    gain, add = pl.pallas_call(
        first_local_kernel,
        out_shape=[jax.ShapeDtypeStruct((LOW * 8, LOW), jnp.float32)] * 2,
        scratch_shapes=[pltpu.VMEM((16, 32, 256), jnp.float32)],
        compiler_params=pltpu.CompilerParams(vmem_limit_bytes=16 * 2**20),
        cost_estimate=pl.CostEstimate(flops=3 * 10**9, bytes_accessed=4 * 2**20, transcendentals=0),
    )(
        field, coupling, advect[:, np.array(B_NODES)], trace, came, links,
        jnp.asarray(stacked3(near, 1)), bf(pick_b),
    )

    lanes = advect[:, np.array(B_NODES + I_NODES)].reshape(2, 2, 32, 2, LOW)
    lanes = lanes.transpose(0, 4, 1, 3, 2).reshape(2, LOW, LOW)
    own = lax.dynamic_slice_in_dim(lanes, 4 * lax.axis_index("span"), 4, axis=1)
    own_inner = jnp.concatenate([own[0, :, 64:], own[1, :, 64:]], axis=1)

    arrived, gain, add, own, own_inner = lax.optimization_barrier((arrived, gain, add, own, own_inner))
    edge, inner = call(first_filter_kernel, [((32, 4, 8, LOW), jnp.float32)] * 2, 10**9)(arrived, high, low)
    edge_back = exchange(edge.reshape(LOW * 8, LOW))

    slope_inner = np.concatenate([slope_a[:, 64:], slope_b[:, 64:]], axis=1)
    inner = call(first_inner_kernel, [((32, 4, 8, LOW), jnp.float32)], 5 * 10**8)(
        arrived, inner, jnp.asarray(stacked3(slope_inner, 0)), own_inner
    )

    edge = edge_back * gain + add
    edge_there = exchange(edge).reshape(32, 4, 8, LOW)

    trace, out = call(
        second_traces_kernel, [((128, 1024), jnp.float32), ((64, 128), jnp.float32)], 5 * 10**8
    )(edge, picks)
    came = travelled(out)
    lift = call(second_local_kernel, [((16, 32, 256), jnp.float32)], 10**9)(trace, came, links)

    slope = np.concatenate([slope_a, slope_b], axis=1)
    edge_there, lift = lax.optimization_barrier((edge_there, lift))
    value = call(second_filter_kernel, [((32, 4, 16, LOW), jnp.float32)], 2 * 10**9)(
        edge_there, inner, high, low, jnp.asarray(stacked3(slope, 0)), own,
        jnp.asarray(PEN * count[None, :], jnp.float32),
    )
    value = exchange(value.reshape(LOW * 16, LOW))
    return call(final_kernel, [((16, 64, 256), jnp.float32)], 2 * 10**8)(value, lift, bf(order.T))


def solution(mesh):
    placed = (
        P("span", None, "mesh"),
        P("span", None, "mesh"),
        P(None, None, "mesh"),
        P("mesh", None, None),
        P(None, "mesh"),
    )
    return jax.shard_map(shards, mesh=mesh, in_specs=placed, out_specs=P("span", None, "mesh"), check_vma=False)
```

```python
import functools

import jax
import jax.numpy as jnp
import numpy as np
from jax import lax
from jax.experimental import pallas as pl
from jax.experimental.pallas import tpu as pltpu
from jax.sharding import PartitionSpec as P


NZ = 512
PLANES = 16
PEN = 0.3
LOW = 128

EDGE_B = (
    [(t, 0) for t in range(8)]
    + [(t, 7) for t in range(8)]
    + [(1, 1)] + [(0, t) for t in range(1, 7)] + [(6, 1)]
    + [(1, 6)] + [(7, t) for t in range(1, 7)] + [(6, 6)]
)
B_NODES = [8 * b + a for a, b in EDGE_B]
I_NODES = [n for n in range(64) if n not in B_NODES]


def split_table(table):
    high = table.astype(jnp.bfloat16)
    low = (table - np.asarray(high, np.float64)).astype(jnp.bfloat16)
    return np.asarray(high), np.asarray(low)


def filter_table():
    wave = np.arange(NZ // 2 + 1)
    keep = np.where(3 * wave <= NZ, 1.0 - 0.5 * (2.0 * wave / NZ) ** 2, 0.0)
    fold = np.where((wave == 0) | (wave == NZ // 2), 1.0, 2.0) / NZ
    lag = np.arange(NZ)
    phase = 2.0 * np.pi * ((wave[:, None] * lag[None, :]) % NZ) / NZ
    row = np.sum((keep * fold)[:, None] * np.cos(phase), axis=0)
    return row[(lag[:, None] - lag[None, :]) % NZ]


def derivative_tables():
    index = np.arange(8)
    points = np.cos(np.pi * index / 7.0)
    weights = np.where((index == 0) | (index == 7), 2.0, 1.0) * (-1.0) ** index
    distance = points[:, None] - points[None, :] + np.eye(8)
    matrix = np.outer(weights, 1.0 / weights) / distance * (1.0 - np.eye(8))
    matrix = matrix - np.eye(8) * np.sum(matrix, axis=1)[:, None]
    return np.kron(np.eye(8), matrix), np.kron(matrix, np.eye(8))


def edge_count():
    count = np.zeros(64)
    for n in range(64):
        a, b = n % 8, n // 8
        count[n] = (a == 0) + (a == 7) + (b == 0) + (b == 7)
    return count


def lane_node(lane):
    which, rest = divmod(lane, 64)
    half, i = divmod(rest, 32)
    return half, (B_NODES if which == 0 else I_NODES)[i]


def order_table():
    table = np.zeros((128, 128))
    for lane in range(128):
        half, node = lane_node(lane)
        table[lane, 64 * half + node] = 1.0
    return table


def lane_tables():
    along_a, along_b = derivative_tables()
    out = [np.zeros((128, 128)) for _ in range(2)]
    for k, matrix in enumerate((along_a, along_b)):
        for p in range(128):
            for n in range(128):
                hp, np_ = lane_node(p)
                hn, nn = lane_node(n)
                if hp == hn:
                    out[k][n, p] = matrix[np_, nn]
    count = np.array([edge_count()[lane_node(p)[1]] for p in range(128)])
    return out[0], out[1], count


def iota(shape, axis):
    return lax.broadcasted_iota(jnp.int32, shape, axis)


def halves(x):
    high = x.astype(jnp.bfloat16)
    return high, (x - high.astype(jnp.float32)).astype(jnp.bfloat16)


def dot(a, b):
    return jnp.dot(a, b, preferred_element_type=jnp.float32)


def dot3(ah, al, bh, bl):
    return dot(ah, bh) + dot(ah, bl) + dot(al, bh)


def stack_halves(x):
    return jnp.concatenate([x[:, :LOW], x[:, LOW:]], axis=0)


def call(kernel, outs, flops, limit=16):
    def run(*args):
        moved = sum(a.size * a.dtype.itemsize for a in args)
        moved += sum(int(np.prod(o[0])) * 4 for o in outs)
        shapes = [jax.ShapeDtypeStruct(o[0], o[1]) for o in outs]
        result = pl.pallas_call(
            kernel,
            out_shape=shapes if len(shapes) > 1 else shapes[0],
            compiler_params=pltpu.CompilerParams(vmem_limit_bytes=limit * 2**20),
            cost_estimate=pl.CostEstimate(flops=flops, bytes_accessed=moved, transcendentals=0),
        )(*args)
        return result

    return run


def pack_kernel(field_ref, coupling_ref, order_ref, out_ref):
    order = order_ref[...]
    inner = order[64:]
    for j in range(PLANES):
        c = coupling_ref[j]
        x = stack_halves(field_ref[j] * (1.0 + c))
        xh, xl = halves(x)
        out_ref[pl.ds(j, LOW, stride=24), :] = (dot(order, xh) + dot(order, xl)).T
    for j in range(8):
        parts = []
        for up in (0, 8):
            ch, cl = halves(stack_halves(coupling_ref[j + up]))
            parts.append(dot(inner, ch) + dot(inner, cl))
        out_ref[pl.ds(16 + j, LOW, stride=24), :] = jnp.concatenate(parts, axis=0).T


def one_hot_rows(index_ref, width):
    index = index_ref[...]
    hot = iota((index.shape[0], width), 1) == index
    return jnp.where(hot, 1.0, 0.0).astype(jnp.bfloat16)


def one_hot_cols(index_ref, first, count):
    index = index_ref[...]
    hot = (iota((count, index.shape[1]), 0) + first) == index
    return jnp.where(hot, 1.0, 0.0).astype(jnp.bfloat16)


NT = (((1,), (1,)), ((), ()))


def dot_nt(a, b):
    return lax.dot_general(a, b, NT, preferred_element_type=jnp.float32)


def sent(trace, pick_ref, sent_ref):
    th, tl = halves(trace)
    pick = one_hot_rows(pick_ref, 1024)
    sent_ref[...] = dot_nt(pick, th) + dot_nt(pick, tl)


def first_traces_kernel(field_ref, coupling_ref, pick_ref, trace_ref, sent_ref, mixed):
    for j in range(PLANES):
        x = field_ref[j] * (1.0 + coupling_ref[j])
        mixed[0, pl.ds(64 * j, 64), :] = x[:, :LOW]
        mixed[1, pl.ds(64 * j, 64), :] = x[:, LOW:]
        trace_ref[pl.ds(8 * j, 8), pl.ds(0, 256)] = x[:8]
        trace_ref[pl.ds(8 * j, 8), pl.ds(512, 256)] = x[56:]
    for h in range(2):
        trace_ref[:, pl.ds(256 + LOW * h, LOW)] = mixed[h, pl.ds(7, 128, stride=8), :]
        trace_ref[:, pl.ds(768 + LOW * h, LOW)] = mixed[h, pl.ds(0, 128, stride=8), :]
    sent(trace_ref[...], pick_ref, sent_ref)


def outer_traces(trace_ref, came_ref, link_ref):
    th, tl = halves(trace_ref[...])
    ch, cl = halves(came_ref[...].T)
    here = one_hot_cols(link_ref, 0, 1024)
    there = one_hot_cols(link_ref, 1024, 64)
    return dot(th, here) + dot(tl, here) + dot(ch, there) + dot(cl, there)


def lifted(outer):
    f0, f1, f2, f3 = (outer[:, 256 * f : 256 * f + 256].reshape(16, 8, 256) for f in range(4))
    t = iota((16, 8, 256), 1)
    first, last = t == 0, t == 7
    g0 = f0 + jnp.where(first, f3[:, 0:1], 0.0) + jnp.where(last, f1[:, 0:1], 0.0)
    g1 = f2 + jnp.where(first, f3[:, 7:8], 0.0) + jnp.where(last, f1[:, 7:8], 0.0)
    ends = first | last
    return g0, g1, jnp.where(ends, 0.0, f3), jnp.where(ends, 0.0, f1)


def first_local_kernel(
    field_ref, coupling_ref, advect_ref, trace_ref, came_ref, link_ref, near_ref, pick_ref, gain_ref, add_ref, lift
):
    for g, part in enumerate(lifted(outer_traces(trace_ref, came_ref, link_ref))):
        lift[:, pl.ds(8 * g, 8), :] = part * PEN
    near = near_ref[...]
    pick = pick_ref[...]
    ad_a, ad_b = advect_ref[0], advect_ref[1]

    def plane(j):
        c = coupling_ref[j]
        xh, xl = halves(field_ref[j] * (1.0 + c))
        parts = dot(near, jnp.concatenate([xh, xl, xh], axis=0))
        ch, cl = halves(c)
        gain = 1.0 + (dot(pick, ch) + dot(pick, cl))
        local = ad_a * parts[0:32] + ad_b * parts[32:64] + parts[64:96] + lift[j]
        return gain, gain * local

    for j in range(8):
        gains, adds = [], []
        for up in (0, 8):
            gain, add = plane(j + up)
            gains.append(stack_halves(gain))
            adds.append(stack_halves(add))
        gain_ref[pl.ds(j, LOW, stride=8), :] = jnp.concatenate(gains, axis=0).T
        add_ref[pl.ds(j, LOW, stride=8), :] = jnp.concatenate(adds, axis=0).T


def second_traces_kernel(value_ref, pick_ref, trace_ref, sent_ref):
    t = iota((8, 256), 0)
    for j in range(8):
        rows = value_ref[pl.ds(j, LOW, stride=8), :].T
        for up in range(2):
            part = rows[64 * up : 64 * up + 64]
            g = [
                jnp.concatenate([part[8 * k : 8 * k + 8], part[32 + 8 * k : 40 + 8 * k]], axis=1) for k in range(4)
            ]
            f3 = jnp.where(t == 0, g[0][0:1], jnp.where(t == 7, g[1][0:1], g[2]))
            f1 = jnp.where(t == 0, g[0][7:8], jnp.where(t == 7, g[1][7:8], g[3]))
            for f, one in enumerate((g[0], f1, g[1], f3)):
                trace_ref[pl.ds(8 * (j + 8 * up), 8), pl.ds(256 * f, 256)] = one
    sent(trace_ref[...], pick_ref, sent_ref)


def second_local_kernel(trace_ref, came_ref, link_ref, lift_ref):
    for g, part in enumerate(lifted(outer_traces(trace_ref, came_ref, link_ref))):
        lift_ref[:, pl.ds(8 * g, 8), :] = part * PEN


def final_kernel(value_ref, lift_ref, back_ref, out_ref):
    back = back_ref[...]
    for j in range(PLANES):
        rows = value_ref[pl.ds(j, LOW, stride=16), :].T
        edge = rows[:64] + stack_halves(lift_ref[j])
        rows = jnp.concatenate([edge, rows[64:]], axis=0)
        rh, rl = halves(rows)
        full = dot(back, rh) + dot(back, rl)
        out_ref[j] = jnp.concatenate([full[:64], full[64:]], axis=1)


def lanes_swapped(x):
    return pltpu.roll(x, 64, x.ndim - 1)


def first_filter_kernel(value_ref, high_ref, low_ref, edge_ref, inner_ref):
    low_lanes = iota((32, 8, LOW), 2) < 64
    for pair in range(2):
        xs = [value_ref[:, 2 * pair + k, pl.ds(0, 16), :].reshape(NZ, LOW) for k in range(2)]
        xh, xl = halves(jnp.concatenate(xs, axis=1))
        y = dot3(high_ref[...], low_ref[...], xh, xl)
        for k in range(2):
            e = 2 * pair + k
            rows = y[:, LOW * k : LOW * k + LOW].reshape(32, 16, LOW)
            up, down = rows[:, :8], rows[:, 8:]
            edge_ref[:, e] = jnp.where(low_lanes, up, lanes_swapped(down.reshape(256, LOW)).reshape(32, 8, LOW))
            inner_ref[:, e] = jnp.where(low_lanes, lanes_swapped(up.reshape(256, LOW)).reshape(32, 8, LOW), down)


def first_inner_kernel(value_ref, inner_ref, slope_ref, advect_ref, out_ref):
    low_lanes = iota((32, 8, LOW), 2) < 64
    slope = slope_ref[...]
    for e in range(4):
        xh, xl = halves(value_ref[:, e, pl.ds(0, 16), :].reshape(NZ, LOW))
        u = dot(jnp.concatenate([xh, xl, xh], axis=1), slope) * advect_ref[pl.ds(e, 1), :]
        v = (u + lanes_swapped(u)).reshape(32, 16, LOW)
        local = jnp.where(low_lanes, v[:, :8], v[:, 8:])
        out_ref[:, e] = (inner_ref[:, e] + local) * (1.0 + value_ref[:, e, pl.ds(16, 8), :])


def second_filter_kernel(edge_ref, inner_ref, high_ref, low_ref, slope_ref, advect_ref, count_ref, out_ref):
    low_lanes = iota((32, 8, LOW), 2) < 64
    slope = slope_ref[...]
    count = count_ref[...]
    for pair in range(2):
        xs = []
        for k in range(2):
            e = 2 * pair + k
            edge, inner = edge_ref[:, e], inner_ref[:, e]
            up = jnp.where(low_lanes, edge, lanes_swapped(inner.reshape(256, LOW)).reshape(32, 8, LOW))
            down = jnp.where(low_lanes, lanes_swapped(edge.reshape(256, LOW)).reshape(32, 8, LOW), inner)
            xs.append(jnp.concatenate([up, down], axis=1).reshape(NZ, LOW))
        xh, xl = halves(jnp.concatenate(xs, axis=1))
        y = dot3(high_ref[...], low_ref[...], xh, xl)
        for k in range(2):
            e = 2 * pair + k
            lanes = slice(LOW * k, LOW * k + LOW)
            u = dot(jnp.concatenate([xh[:, lanes], xl[:, lanes], xh[:, lanes]], axis=1), slope)
            z = y[:, lanes] + u[:, :LOW] * advect_ref[0, pl.ds(e, 1), :] + u[:, LOW:] * advect_ref[1, pl.ds(e, 1), :]
            z = z - xs[k] * count
            out_ref[:, e] = z.reshape(32, 16, LOW)


def stacked3(table, axis):
    high, low = split_table(table)
    return np.concatenate([high, high, low], axis=axis)


def exchange(x):
    return lax.all_to_all(x, "span", split_axis=0, concat_axis=0, tiled=True)


def shifted(block, distance):
    devices = lax.axis_size("mesh")
    return lax.ppermute(block, "mesh", [((i - distance) % devices, i) for i in range(devices)])


def link_tables(send_rows, neighbours):
    elems = neighbours.shape[1]
    capacity = send_rows.shape[2]
    count = lax.axis_size("mesh")
    here = lax.axis_index("mesh")
    before, after = (here - 1) % count, (here + 1) % count

    def lane(v):
        return (v % 4) * elems + v // 4

    def rows(peer):
        chosen = lax.dynamic_index_in_dim(send_rows[0], peer, 0, keepdims=False)
        return jnp.pad(lane(chosen), (0, 32 - capacity))

    picks = jnp.concatenate([rows(after), rows(before)])[:, None]
    links = neighbours.reshape(1, 4 * elems)
    offset = links - 4 * elems
    peer, within = offset // capacity, offset % capacity
    index = jnp.where(
        links < 4 * elems,
        lane(links),
        jnp.where(peer == before, 4 * elems + within, jnp.where(peer == after, 4 * elems + 32 + within, -1)),
    )
    return picks.astype(jnp.int32), index.astype(jnp.int32)


def travelled(out):
    return jnp.concatenate([shifted(out[:32], 1), shifted(out[32:], -1)], axis=0)


def shards(field, coupling, advect, send_rows, neighbours):
    high, low = split_table(filter_table())
    order = order_table()
    slope_a, slope_b, count = lane_tables()
    along_a, along_b = derivative_tables()
    pick_b = np.eye(64)[B_NODES]
    near = np.concatenate(
        [along_a[B_NODES], along_b[B_NODES], -PEN * edge_count()[B_NODES][:, None] * pick_b], axis=0
    )
    bf = lambda t: jnp.asarray(t, jnp.bfloat16)
    high, low = jnp.asarray(high), jnp.asarray(low)

    packed = call(pack_kernel, [((LOW * 24, LOW), jnp.float32)], 2 * 10**8, 60)(field, coupling, bf(order))
    arrived = exchange(packed).reshape(32, 4, 24, LOW)

    picks, links = link_tables(send_rows, neighbours)
    trace, out = pl.pallas_call(
        first_traces_kernel,
        out_shape=[jax.ShapeDtypeStruct((128, 1024), jnp.float32), jax.ShapeDtypeStruct((64, 128), jnp.float32)],
        scratch_shapes=[pltpu.VMEM((2, 1024, LOW), jnp.float32)],
        compiler_params=pltpu.CompilerParams(vmem_limit_bytes=16 * 2**20),
        cost_estimate=pl.CostEstimate(flops=10**9, bytes_accessed=3 * 2**20, transcendentals=0),
    )(field, coupling, picks)
    came = travelled(out)
    gain, add = pl.pallas_call(
        first_local_kernel,
        out_shape=[jax.ShapeDtypeStruct((LOW * 8, LOW), jnp.float32)] * 2,
        scratch_shapes=[pltpu.VMEM((16, 32, 256), jnp.float32)],
        compiler_params=pltpu.CompilerParams(vmem_limit_bytes=16 * 2**20),
        cost_estimate=pl.CostEstimate(flops=3 * 10**9, bytes_accessed=4 * 2**20, transcendentals=0),
    )(
        field, coupling, advect[:, np.array(B_NODES)], trace, came, links,
        jnp.asarray(stacked3(near, 1)), bf(pick_b),
    )

    lanes = advect[:, np.array(B_NODES + I_NODES)].reshape(2, 2, 32, 2, LOW)
    lanes = lanes.transpose(0, 4, 1, 3, 2).reshape(2, LOW, LOW)
    own = lax.dynamic_slice_in_dim(lanes, 4 * lax.axis_index("span"), 4, axis=1)
    own_inner = jnp.concatenate([own[0, :, 64:], own[1, :, 64:]], axis=1)

    arrived, gain, add, own, own_inner = lax.optimization_barrier((arrived, gain, add, own, own_inner))
    edge, inner = call(first_filter_kernel, [((32, 4, 8, LOW), jnp.float32)] * 2, 10**9)(arrived, high, low)
    edge_back = exchange(edge.reshape(LOW * 8, LOW))

    slope_inner = np.concatenate([slope_a[:, 64:], slope_b[:, 64:]], axis=1)
    inner = call(first_inner_kernel, [((32, 4, 8, LOW), jnp.float32)], 5 * 10**8)(
        arrived, inner, jnp.asarray(stacked3(slope_inner, 0)), own_inner
    )

    edge = edge_back * gain + add
    edge_there = exchange(edge).reshape(32, 4, 8, LOW)

    trace, out = call(
        second_traces_kernel, [((128, 1024), jnp.float32), ((64, 128), jnp.float32)], 5 * 10**8
    )(edge, picks)
    came = travelled(out)
    lift = call(second_local_kernel, [((16, 32, 256), jnp.float32)], 10**9)(trace, came, links)

    slope = np.concatenate([slope_a, slope_b], axis=1)
    edge_there, lift = lax.optimization_barrier((edge_there, lift))
    value = call(second_filter_kernel, [((32, 4, 16, LOW), jnp.float32)], 2 * 10**9)(
        edge_there, inner, high, low, jnp.asarray(stacked3(slope, 0)), own,
        jnp.asarray(PEN * count[None, :], jnp.float32),
    )
    value = exchange(value.reshape(LOW * 16, LOW))
    return call(final_kernel, [((16, 64, 256), jnp.float32)], 2 * 10**8)(value, lift, bf(order.T))


def solution(mesh):
    placed = (
        P("span", None, "mesh"),
        P("span", None, "mesh"),
        P(None, None, "mesh"),
        P("mesh", None, None),
        P(None, "mesh"),
    )
    return jax.shard_map(shards, mesh=mesh, in_specs=placed, out_specs=P("span", None, "mesh"), check_vma=False)
```
